128 devices in a mesh: shard: 16 (over x_hi, y, core), rep: 8 (over x_lo, z).
Axes of the slice: x: 4 (x_hi: 2, x_lo: 2; x = x_hi * 2 + x_lo), y: 4, z: 4, core: 2. Of those that a mesh axis runs over, the one named last changes fastest.
Arguments:
- layer_input: bfloat16 [16, 1024, 1024], P('shard', 'rep'), may hold values from -6 to 6
- cotangent: bfloat16 [16, 1024, 1024], P('shard', 'rep'), may hold values from -6 to 6
- gain_attn: bfloat16 [1024], P('shard'), may hold values from 0.5 to 1.5
- w_query: bfloat16 [1024, 1024], P('shard'), may hold values from -0.1875 to 0.1875
- w_keyval: bfloat16 [1024, 1024], P('shard'), may hold values from -0.1875 to 0.1875
- w_output: bfloat16 [1024, 1024], P('shard'), may hold values from -1.5 to 1.5
- gain_moe: bfloat16 [1024], P('shard'), may hold values from 0.5 to 1.5
- w_router: bfloat16 [1024, 32], P('shard'), may hold values from -0.125 to 0.125
- w_in: bfloat16 [32, 1024, 1024], P('shard'), may hold values from -0.1875 to 0.1875
- w_out: bfloat16 [32, 512, 1024], P('shard'), may hold values from -1 to 1
- routes: int32 [16, 1024, 8], P('shard', 'rep'), may hold values from 0 to 31, all different within a row
- priority: int32 [16, 8, 128], P('shard', 'rep'), may hold values from 0 to 127, each once within a row
- block_ids: int32 [16, 1024], P('shard', 'rep'), may hold values from 0 to 7, never falling along the last dimension, each value on 1 to 256 neighbouring positions
Outputs:
- result: bfloat16 [16, 1024, 1024], P('shard', 'rep')
- grad_input: float32 [16, 1024, 1024], P('shard', 'rep')
- grad_gain_attn: float32 [1024], P('shard')
- grad_query: float32 [1024, 1024], P('shard')
- grad_keyval: float32 [1024, 1024], P('shard')
- grad_output: float32 [1024, 1024], P('shard')
- grad_gain_moe: float32 [1024], P('shard')
- grad_router: float32 [1024, 32], P('shard')
- grad_in: float32 [32, 1024, 1024], P('shard', 'rep')
- grad_out: float32 [32, 512, 1024], P('shard', 'rep')
The draws below stay inside these ranges and needn't reach their ends.
Inputs may be any that keep to these rules, and one draw needn't show every extreme that they name: `routes`: the 8 experts of a token differ. `priority`: each device's 128 entries are a permutation. `block_ids`: never falling along a sequence; a block has 1 to 256 tokens, one exactly 256.
All inputs are finite; a program needn't handle non-finite values.
Results may differ from the reference program's by a relative error of at most 0.028.
Values may be sent and summed in bfloat16 or wider, within the bound.
No kernel may reach another device: no remote copies, remote signals or barrier semaphores. Data moves between devices by JAX's collectives and lax.ppermute only.
A program may use at most 192 MiB of HBM per device.

```python
import math
import jax
import jax.numpy as jnp
import numpy as np
from jax import lax

D = 1024
HEADS = 16
KV = 8
HD = 64
F = 512
EXPERTS = 32
TOPK = 8
TOK_DEV = 128
BLK = 256
LEN = 1024
SEQS = 16
CAP = 40
N_REP = 8


def levels(own_key, shape, split, smallest, largest):
    def one(position, shards_of):
        steps = jax.random.uniform(jax.random.fold_in(jax.random.fold_in(own_key, 6), position), (shards_of,), jnp.float32, smallest / len(split), largest / len(split))
        return jnp.repeat(jnp.exp(steps), shape[position] // shards_of).reshape((-1,) + (1,) * (len(shape) - position - 1))

    gain = one(*split[0])
    for cut in split[1:]:
        gain = gain * one(*cut)
    return gain


def picks_of(rng, rows, count, top, lift):
    sequence = jax.random.permutation(jax.random.fold_in(rng, 1), count)
    pull = sequence
    for power in range(3):
        pull = pull * pull // count
    pull = pull * lift // count
    chance = jax.random.randint(jax.random.fold_in(rng, 2), (rows, count), 0, 4096) + pull
    sure = jax.random.permutation(jax.random.fold_in(rng, 3), rows)[jnp.arange(count) % rows]
    chance = jnp.where(jnp.arange(rows)[:, None] == sure[None, :], 1 << 14, chance)
    score = chance * count + jnp.arange(count)
    return lax.top_k(score.astype(jnp.int32), top)[1].astype(jnp.int32)


def length_profile(count, total, reach, slope):
    portions = [(1 << 20) // math.isqrt(rank ** slope) + 1 for rank in range(2, count + 1)]
    surplus, counts = total - reach - (count - 1), [1] * (count - 1)
    while surplus > 0:
        candidates = [i for i in range(count - 1) if counts[i] < reach]
        pool, budget = sum([portions[i] for i in candidates]), surplus
        for i in candidates:
            extra = min(reach - counts[i], max(1, budget * portions[i] // pool), surplus)
            counts[i] = counts[i] + extra
            surplus = surplus - extra
    return np.array([reach] + counts)


def uneven(rng, amount, total, limit, slope):
    if amount == 2:
        one = jax.random.randint(rng, (), max(1, total - limit), min(limit, total - 1) + 1)
        return jnp.stack([one, total - one])
    lengths = jnp.asarray(length_profile(amount, total, limit, slope), jnp.int32)
    pairs = (amount - 1) // 2
    source_of, sink = lengths[1:1 + 2 * pairs:2], lengths[2:2 + 2 * pairs:2]
    margin = jnp.minimum(source_of - 1, limit - sink)
    moved = jax.random.randint(jax.random.fold_in(rng, 1), (pairs,), 0, 1 << 20) % (margin + 1)
    lengths = lengths.at[1:1 + 2 * pairs:2].set(source_of - moved).at[2:2 + 2 * pairs:2].set(sink + moved)
    return lengths[jax.random.permutation(jax.random.fold_in(rng, 2), amount)]


def noise(stream_key, extent, deviation, bound, shards=(), held_as=jnp.bfloat16):
    level = levels(stream_key, extent, shards, -0.22, 0.18) if shards else 1.0
    array = jax.random.normal(stream_key, extent, jnp.float32) * deviation * level
    return jnp.minimum(jnp.maximum(array, -bound), bound).astype(held_as)


def setup_inputs(seed: int = 0) -> dict:
    keys = jax.random.split(jax.random.key(seed), 14)
    layer_input = noise(keys[0], (SEQS, LEN, D), 1.0, 6.0, ((0, 16), (1, 8)))
    cotangent = noise(keys[1], (SEQS, LEN, D), 1.0, 6.0, ((0, 16), (1, 8)))
    gain_attn = jnp.clip(1.0 + 0.1 * jax.random.normal(keys[2], (D,), jnp.float32), 0.5, 1.5).astype(jnp.bfloat16)
    w_query = noise(keys[3], (D, HEADS * HD), D ** -0.5, 0.1875, ((0, 16),))
    w_keyval = noise(keys[4], (D, 2 * KV * HD), D ** -0.5, 0.1875, ((0, 16),))
    w_output = noise(keys[5], (HEADS * HD, D), 0.25, 1.5, ((0, 16),))
    gain_moe = jnp.clip(1.0 + 0.1 * jax.random.normal(keys[6], (D,), jnp.float32), 0.5, 1.5).astype(jnp.bfloat16)
    w_router = noise(keys[7], (D, EXPERTS), 0.02, 0.125, ((0, 16),))
    w_in = noise(keys[8], (EXPERTS, D, 2 * F), D ** -0.5, 0.1875, ((0, 16),))
    w_out = noise(keys[9], (EXPERTS, F, D), (F // 16) ** -0.5, 1.0, ((0, 16),))
    routes = picks_of(keys[10], SEQS * LEN, EXPERTS, TOPK, 2048).reshape((SEQS, LEN, TOPK))
    priority = jax.vmap(lambda own: jax.random.permutation(own, TOK_DEV))(jax.random.split(keys[11], SEQS * N_REP)).reshape((SEQS, N_REP, TOK_DEV)).astype(jnp.int32)
    block_ids = jax.vmap(lambda own: jnp.searchsorted(jnp.cumsum(uneven(own, 2 * LEN // BLK, LEN, BLK, 0)), jnp.arange(LEN), side="right"))(jax.random.split(keys[12], SEQS)).reshape((SEQS, LEN)).astype(jnp.int32)
    return {"layer_input": layer_input, "cotangent": cotangent, "gain_attn": gain_attn, "w_query": w_query, "w_keyval": w_keyval, "w_output": w_output, "gain_moe": gain_moe, "w_router": w_router, "w_in": w_in, "w_out": w_out, "routes": routes, "priority": priority, "block_ids": block_ids}


@jax.custom_vjp
def low(v):
    return lax.optimization_barrier(v.astype(jnp.bfloat16)).astype(jnp.float32)

@jax.custom_vjp
def low_back(v):
    return v

def low_keep(v):
    return (low(v), None)

def low_pass(kept, grad):
    return (grad,)

def back_keep(v):
    return (v, None)

def back_low(kept, grad):
    return (low(grad),)
low.defvjp(low_keep, low_pass)
low_back.defvjp(back_keep, back_low)
epsilon = 1e-06
highest = lax.Precision.HIGHEST

def product(first_op, second_op):
    return jnp.dot(first_op, second_op, precision=highest, preferred_element_type=jnp.float32)

def rms_apply(values, scaling):
    return values * lax.rsqrt(lax.optimization_barrier(jnp.mean(values * values, axis=-1, keepdims=True)) + epsilon) * scaling

def rotate(values, positions):
    halfway = values.shape[-1] // 2
    exponent = jnp.arange(halfway, dtype=jnp.float32) * (-2.0 / values.shape[-1])
    frequency = jnp.power(10000.0, exponent)
    angles = positions.astype(jnp.float32)[:, None] * frequency[None, :]
    cosine = jnp.cos(angles)[:, None, :]
    sine_part = jnp.sin(angles)[:, None, :]
    first_half = values[..., :halfway]
    second_half = values[..., halfway:]
    return jnp.concatenate([first_half * cosine - second_half * sine_part, second_half * cosine + first_half * sine_part], axis=-1)

def swiglu(hidden_pre):
    middle = hidden_pre.shape[-1] // 2
    return jax.nn.silu(hidden_pre[..., :middle]) * hidden_pre[..., middle:]

def slot_tables(routes, priority):
    count_tokens, top_count = routes.shape
    chosen = routes[:, :, None] == jnp.arange(EXPERTS, dtype=jnp.int32)[None, None, :]
    member = lax.optimization_barrier(jnp.sum(chosen, axis=1)).astype(jnp.float32)
    earlier = (priority[None, :] < priority[:, None]).astype(jnp.float32)
    before = jnp.dot(earlier, member, precision=highest, preferred_element_type=jnp.float32)
    ranking = lax.optimization_barrier(jnp.sum(jnp.where(chosen, before[:, None, :], 0.0), axis=2)).astype(jnp.int32)
    slot_index = jnp.where(ranking < CAP, routes * CAP + ranking, EXPERTS * CAP)
    owners = jnp.full((EXPERTS * CAP + 1,), count_tokens, jnp.int32)
    owners = owners.at[slot_index.reshape(-1)].set(jnp.repeat(jnp.arange(count_tokens, dtype=jnp.int32), top_count))
    return (slot_index, owners[:EXPERTS * CAP])

def forward(inputs, gain_attn, w_query, w_keyval, w_output, gain_moe, w_router, w_in, w_out, routes, priority, block_ids):
    normed = low(rms_apply(inputs, gain_attn))
    query_pre = low_back(product(normed, w_query))
    keyval_pre = low_back(product(normed, w_keyval))
    positions = jnp.arange(LEN, dtype=jnp.int32)
    score_scale = HD ** (-0.5)

    def attend(pieces):
        query_seq, keyval_seq, block_seq = pieces
        queries = low(rotate(query_seq.reshape(LEN, HEADS, HD), positions)).reshape(LEN, KV, HEADS // KV, HD)
        key_rows = low(rotate(keyval_seq[:, :KV * HD].reshape(LEN, KV, HD), positions))
        value_rows = low(keyval_seq[:, KV * HD:].reshape(LEN, KV, HD))
        scores = jnp.einsum('tgrd,ngd->grtn', queries, key_rows, precision=highest) * score_scale
        visible = block_seq[None, :] <= block_seq[:, None]
        scores = low_back(jnp.where(visible[None, None], scores, -1e+30))
        attention_weights = jax.nn.softmax(scores, axis=-1)
        mixture = jnp.einsum('grtn,ngd->tgrd', low(attention_weights), value_rows, precision=highest)
        return mixture.reshape(LEN, HEADS * HD)
    attended = lax.map(jax.checkpoint(attend), (query_pre, keyval_pre, block_ids))
    attended = low(low_back(attended))
    hidden = inputs + low_back(product(attended, w_output))
    normed_moe = low(rms_apply(hidden, gain_moe))
    group_count = SEQS * N_REP

    def route_group(pieces):
        group_rows, group_routes, group_priority = pieces
        logits = low_back(product(group_rows, w_router))
        gate_values = jax.nn.softmax(jnp.take_along_axis(logits, group_routes, axis=1), axis=-1)
        slot_index, owners = slot_tables(group_routes, group_priority)
        padded = jnp.concatenate([group_rows, jnp.zeros((1, D), group_rows.dtype)], axis=0)
        dispatched = padded[owners].reshape(EXPERTS, CAP, D)
        pre_act = low_back(jnp.einsum('ecd,edf->ecf', dispatched, w_in, precision=highest))
        outputs = low_back(jnp.einsum('ecf,efd->ecd', low(swiglu(pre_act)), w_out, precision=highest))
        outputs = jnp.concatenate([outputs.reshape(EXPERTS * CAP, D), jnp.zeros((1, D), outputs.dtype)], axis=0)
        return lax.optimization_barrier(jnp.sum(gate_values[:, :, None] * outputs[slot_index], axis=1))
    expert_sum = lax.map(jax.checkpoint(route_group), (normed_moe.reshape(group_count, TOK_DEV, D), routes.reshape(group_count, TOK_DEV, TOPK), priority.reshape(group_count, TOK_DEV)))
    return hidden + expert_sum.reshape(SEQS, LEN, D)

def reference(layer_input, cotangent, gain_attn, w_query, w_keyval, w_output, gain_moe, w_router, w_in, w_out, routes, priority, block_ids):
    floats = (layer_input, gain_attn, w_query, w_keyval, w_output, gain_moe, w_router, w_in, w_out)
    floats = tuple((member_array.astype(jnp.float32) for member_array in floats))

    def layer_fn(*arrays):
        return forward(*arrays, routes, priority, block_ids)
    result, pullback = jax.vjp(layer_fn, *floats)
    gradients = pullback(cotangent.astype(jnp.float32))
    return (result.astype(jnp.bfloat16), gradients[0], gradients[1], gradients[2], gradients[3], gradients[4], gradients[5], gradients[6], gradients[7], gradients[8])
```

```python
import itertools
import math

import jax
import jax.numpy as jnp
import numpy as np
from jax import lax
from jax.experimental import pallas as pl
from jax.experimental.pallas import tpu as pltpu
from jax.sharding import Mesh
from jax.sharding import PartitionSpec as P

HEADS = 16
KV = 8
HD = 64
EXPERTS = 32
TOPK = 8
CAP = 40
TOK = 128
D = 1024
F = 512
LEN = 1024
EPS = 1e-06
SHARD = ("xh", "y", "c")
REP = ("xl", "z")
SIZES = {"xh": 2, "y": 4, "c": 2, "xl": 2, "z": 4}
bf16 = jnp.bfloat16
f32 = jnp.float32

VM = pl.BlockSpec(memory_space=pltpu.VMEM)
SM = pl.BlockSpec(memory_space=pltpu.SMEM)


def moved(x, axes, to):
    sizes = [SIZES[a] for a in axes]
    pairs = []
    for here in itertools.product(*[range(s) for s in sizes]):
        there = to(*here)
        a = b = 0
        for s, i, j in zip(sizes, here, there):
            a, b = a * s + i, b * s + j % s
        pairs.append((a, b))
    return lax.ppermute(x, axes, pairs)


def ring(x, axis, sign):
    if axis == "y":
        return moved(x, ("y", "c"), lambda y, c: (y + sign * (1 - 2 * c), c))
    return moved(x, ("c", "z"), lambda c, z: (c, z + sign * (1 - 2 * c)))


def cross(x, axis):
    return moved(x, (axis,), lambda i: (1 - i,))


def spread(x, pair, axis):
    across = cross(x, pair)
    a = ring(x, axis, 1)
    b = ring(x, axis, -1)
    xa = ring(across, axis, 1)
    xb = ring(across, axis, -1)
    a2 = ring(a, axis, 1)
    xa2 = ring(xa, axis, 1)
    return [x, a, b, a2, across, xa, xb, xa2]


def owners(pair, axis, core):
    i, j = lax.axis_index(pair), lax.axis_index(axis)
    way = 1 - 2 * core
    steps = (0, -1, 1, -2)
    return [p * 4 + (j + s * way) % 4 for p in (i, 1 - i) for s in steps]


def plus(*terms):
    total = terms[0].astype(f32)
    for t in terms[1:]:
        total = total + t.astype(f32)
    return total.astype(bf16)


def collect(p, pair, axis):
    r2 = ring(p[7], axis, -1)
    rb = ring(p[6], axis, 1)
    s2 = ring(p[3], axis, -1)
    sb = ring(p[2], axis, 1)
    ra = ring(plus(p[5], r2), axis, -1)
    sa = ring(plus(p[1], s2), axis, -1)
    rv = cross(plus(p[4], rb, ra), pair)
    return [p[0], sb, sa, rv]


def nn(a, b):
    return jnp.dot(a, b, preferred_element_type=f32)


def nt(a, b):
    return lax.dot_general(a, b, (((1,), (1,)), ((), ())), preferred_element_type=f32)


def tn(a, b):
    return lax.dot_general(a, b, (((0,), (0,)), ((), ())), preferred_element_type=f32)


def lanes(shape):
    return lax.broadcasted_iota(jnp.int32, shape, len(shape) - 1)


def rows(shape):
    return lax.broadcasted_iota(jnp.int32, shape, 0)


def call(kernel, name, scalars, arrays, outs, scratch=(), flops=0, vmem=56):
    moved_bytes = sum(a.size * a.dtype.itemsize for a in (*arrays, *outs))
    return pl.pallas_call(
        kernel,
        name=name,
        out_shape=outs,
        in_specs=[SM] * len(scalars) + [VM] * len(arrays),
        out_specs=[VM] * len(outs),
        scratch_shapes=list(scratch),
        compiler_params=pltpu.CompilerParams(vmem_limit_bytes=vmem << 20),
        cost_estimate=pl.CostEstimate(
            flops=flops, bytes_accessed=moved_bytes, transcendentals=0
        ),
    )(*scalars, *arrays)


def struct(shape, dtype):
    return jax.ShapeDtypeStruct(shape, dtype)


def rope_tables():
    half = HD // 2
    frequency = np.power(10000.0, np.arange(half) * (-2.0 / HD))
    angles = np.arange(LEN)[:, None] * frequency[None, :]
    cosine, sine = np.cos(angles), np.sin(angles)
    return (
        np.concatenate([cosine] * 4, axis=1).astype(np.float32),
        np.concatenate([-sine, sine, -sine, sine], axis=1).astype(np.float32),
    )


def halves_swapped(x):
    first = lanes(x.shape) % HD < HD // 2
    return jnp.where(first, pltpu.roll(x, 96, 1), pltpu.roll(x, 32, 1))


def block_column(marks, j):
    return jnp.transpose(jnp.broadcast_to(marks[j : j + 1, :], (TOK, TOK)))[:, 0:1]


QB = 256


def visible_of(marks, i):
    reach = min(LEN, QB * (i + 2))
    row = jnp.concatenate([marks[j : j + 1, :] for j in range(reach // TOK)], axis=1)
    col = jnp.concatenate(
        [block_column(marks, j) for j in range(QB // TOK * i, QB // TOK * (i + 1))], axis=0
    )
    return reach, row <= col


def attend(rho, w, cos, sin, *refs):
    xs, marks_in = refs[:8], refs[8:16]
    norm, q_out, kv_out, attn_out, low_out, lse_out, gain_out, marks = refs[16:24]
    for j in range(8):
        part = jnp.transpose(w[TOK * j : TOK * (j + 1), 256:384].astype(f32))
        gain_out[0:8, TOK * j : TOK * (j + 1)] = part[32:40, :]
    gain = gain_out[0:1, :]
    for k in range(8):
        at = rho[k]
        marks[pl.ds(at, 1), :] = marks_in[k][...].astype(f32)
        x = xs[k][...].astype(f32)
        inv = lax.rsqrt(jnp.mean(x * x, axis=-1, keepdims=True) + EPS)
        norm[pl.ds(pl.multiple_of(at * TOK, TOK), TOK), :] = (x * inv * gain).astype(bf16)
    pre = nn(norm[...], w[:, 0:256])
    c, s = cos[...], sin[...]
    q = pre[:, 0:128]
    q_out[...] = ((q * c + halves_swapped(q) * s) * (HD**-0.5)).astype(bf16)
    kv = pre[:, 128:256]
    is_key = lanes(kv.shape) < HD
    kv_out[...] = jnp.where(is_key, kv * c + halves_swapped(kv) * s, kv).astype(bf16)
    kvf = kv_out[...].astype(f32)
    turned = pltpu.roll(kvf, HD, 1)
    keys = jnp.where(is_key, kvf, turned).astype(bf16)
    values = jnp.where(is_key, turned, kvf).astype(bf16)
    for i in range(LEN // QB):
        reach, visible = visible_of(marks, i)
        at = slice(QB * i, QB * (i + 1))
        qi = q_out[at, :]
        first = lanes(qi.shape) < HD
        mixed, logs = [], []
        for h in range(2):
            qh = jnp.where(first == (h == 0), qi, jnp.zeros_like(qi))
            scores = jnp.where(visible, nt(qh, keys[:reach]), -1e30)
            top = jnp.max(scores, axis=-1, keepdims=True)
            e = jnp.exp(scores - top)
            total = jnp.sum(e, axis=-1, keepdims=True)
            mixed.append(nn(e.astype(bf16), values[:reach]) / total)
            logs.append(top + jnp.log(total))
        attn = jnp.where(first, mixed[0], mixed[1])
        attn_out[at, :] = attn
        low_out[at, :] = attn.astype(bf16)
        lse_out[at, :] = jnp.where(first, logs[0], logs[1])


def attend_back(rho, cos, sin, q, kv, attn, lse, grad, *refs):
    marks_in, (out, marks, dk, dv) = refs[:8], refs[8:]
    for k in range(8):
        marks[pl.ds(rho[k], 1), :] = marks_in[k][...].astype(f32)
    kvf = kv[...].astype(f32)
    is_key = lanes(kvf.shape) < HD
    turned = pltpu.roll(kvf, HD, 1)
    keys = jnp.where(is_key, kvf, turned).astype(bf16)
    values = jnp.where(is_key, turned, kvf).astype(bf16)
    dk[...] = jnp.zeros_like(dk)
    dv[...] = jnp.zeros_like(dv)
    for i in range(LEN // QB):
        reach, visible = visible_of(marks, i)
        at = slice(QB * i, QB * (i + 1))
        qi, gi = q[at, :], grad[at, :]
        first = lanes(qi.shape) < HD
        part = gi.astype(f32) * attn[at, :]
        dq = []
        for h in range(2):
            mine = first == (h == 0)
            qh = jnp.where(mine, qi, jnp.zeros_like(qi))
            gh = jnp.where(mine, gi, jnp.zeros_like(gi))
            delta = jnp.sum(jnp.where(mine, part, 0.0), axis=-1, keepdims=True)
            scores = nt(qh, keys[:reach])
            log = lse[at, HD * h : HD * h + 1]
            weights = jnp.where(visible, jnp.exp(scores - log), 0.0)
            low = (weights * (nt(gh, values[:reach]) - delta)).astype(bf16)
            dq.append(nn(low, keys[:reach]))
            dk[:reach, :] += tn(low, qh)
            dv[:reach, :] += tn(weights.astype(bf16), gh)
        g = jnp.where(first, dq[0], dq[1]) * (HD**-0.5)
        c, s = cos[at, :], sin[at, :]
        out[at, 0:128] = (g * c - halves_swapped(g) * s).astype(bf16)
    key = dk[...]
    key = key + pltpu.roll(key, HD, 1)
    val = dv[...]
    val = val + pltpu.roll(val, HD, 1)
    key = key * cos[...] - halves_swapped(key) * sin[...]
    out[:, 128:256] = jnp.where(is_key, key, val).astype(bf16)


def to_experts(sigma, x, attn, routes, priority, gain, w, *refs):
    wos = refs[:16]
    wo, low, hidden, payload, gates_out = refs[16:21]
    for k in range(16):
        wo[pl.ds(pl.multiple_of(sigma[k] * 64, 64), 64), :] = wos[k][0:64, :]
    for r in range(8):
        low[:, TOK * r : TOK * (r + 1)] = attn[r]
    h = x[...].astype(f32) + nn(low[...], wo[...])
    hidden[...] = h
    inv = lax.rsqrt(jnp.mean(h * h, axis=-1, keepdims=True) + EPS)
    normed = (h * inv * gain[1:2, :]).astype(bf16)
    payload[:, 0:D] = normed
    logits = nn(normed, w[:, 256:384])
    lane = lanes((TOK, TOK))
    member = lane == routes[:, 0:1]
    for k in range(1, TOPK):
        member = member | (lane == routes[:, k : k + 1])
    order = jnp.broadcast_to(priority[...], (TOK, TOK)).astype(f32)
    earlier = (order < jnp.transpose(order)).astype(f32).astype(bf16)
    before = nn(earlier, member.astype(f32).astype(bf16))
    kept = member & (before < CAP)
    top = jnp.max(jnp.where(member, logits, -1e30), axis=-1, keepdims=True)
    e = jnp.where(member, jnp.exp(jnp.where(member, logits - top, 0.0)), 0.0)
    gates = e / jnp.sum(e, axis=-1, keepdims=True)
    gates_out[...] = gates
    high = gates.astype(bf16).astype(f32)
    rank = jnp.where(kept, before, -1.0)
    meta = jnp.where(
        lane < 32,
        rank,
        jnp.where(lane < 64, pltpu.roll(high, 32, 1), pltpu.roll(gates - high, 64, 1)),
    )
    payload[:, D : D + TOK] = jnp.transpose(meta).astype(bf16)


SLOTS = 16 * CAP


def experts(who, w_in, w_out, *refs):
    xs, cs = refs[:16], refs[16:32]
    disp, act_o, pre_g, out_g = refs[32:36]
    own_s, other_s, own_r, other_r = (refs[36 + 8 * n : 44 + 8 * n] for n in range(4))
    meta, picks, cot_rows, gate_col, back, outs, gg = refs[68:]
    first = who[0] * 2
    two = 2 * CAP
    for p in range(8):
        pair = (p, p + 8)
        side = rows((two, 256)) >= CAP
        place = (rows((two, 256)) - jnp.where(side, CAP, 0)).astype(f32)
        here = side == (lanes((two, 256)) >= TOK)
        chosen = []
        for n, k in enumerate(pair):
            meta[TOK * n : TOK * (n + 1), :] = xs[k][:, D : D + TOK].astype(f32)
        for e in range(2):
            def line(offset):
                return jnp.concatenate(
                    [meta[pl.ds(TOK * n + offset + first + e, 1), :] for n in range(2)], axis=1
                )

            pick = jnp.where((line(0) == place) & here, 1.0, 0.0)
            gate_col[e, two * p : two * (p + 1), :] = jnp.sum(
                pick * (line(32) + line(64)), axis=-1, keepdims=True
            )
            chosen.append(pick.astype(bf16))
        pick = jnp.concatenate(chosen, axis=0)
        picks[p] = pick
        x = jnp.concatenate([xs[k][:, 0:D] for k in pair], axis=0)
        found = nn(pick, x).astype(bf16)
        c = jnp.concatenate([cs[k][64:192, :] for k in pair], axis=0)
        cot = nn(pick, c)
        for e in range(2):
            at = slice(two * p, two * (p + 1))
            disp[e, at, :] = found[two * e : two * (e + 1)]
            cot_rows[e, at, :] = cot[two * e : two * (e + 1)].astype(bf16)
            out_g[e, at, :] = (gate_col[e, at, :] * cot[two * e : two * (e + 1)]).astype(bf16)
    for e in range(2):
        pre = nn(disp[e], w_in[e])
        gate, up = pre[:, 0:F], pre[:, F : 2 * F]
        sig = 1.0 / (1.0 + jnp.exp(-gate))
        silu = gate * sig
        act = (silu * up).astype(bf16)
        act_o[e] = act
        out = nn(act, w_out[e])
        g = jnp.sum(out * cot_rows[e].astype(f32), axis=-1, keepdims=True)
        high = g.astype(bf16).astype(f32)
        lane = lanes((SLOTS, TOK))
        gg[e] = jnp.where(
            lane == first + e, high, jnp.where(lane == first + e + 32, g - high, 0.0)
        ).astype(bf16)
        outs[e] = (gate_col[e] * out).astype(bf16)
        act_grad = nt(out_g[e], w_out[e])
        d_up = act_grad * silu
        d_gate = act_grad * up * (sig * (1.0 + gate * (1.0 - sig)))
        pre_g[e, :, 0:F] = d_gate.astype(bf16)
        pre_g[e, :, F : 2 * F] = d_up.astype(bf16)
        back[e] = nt(pre_g[e], w_in[e]).astype(bf16)
    for p in range(8):
        at = slice(two * p, two * (p + 1))
        pick = picks[p]
        slot = jnp.concatenate([back[0, at, :], back[1, at, :]], axis=0)
        grads = jnp.concatenate([gg[0, at, :], gg[1, at, :]], axis=0)
        value = jnp.concatenate([outs[0, at, :], outs[1, at, :]], axis=0)
        total = tn(pick, slot).astype(bf16)
        own_s[p][:, 0:D] = total[0:TOK]
        other_s[p][:, 0:D] = total[TOK:]
        total = tn(pick, grads).astype(bf16)
        own_s[p][:, D : D + TOK] = total[0:TOK]
        other_s[p][:, D : D + TOK] = total[TOK:]
        total = tn(pick, value).astype(bf16)
        own_r[p][...] = total[0:TOK]
        other_r[p][...] = total[TOK:]


def expert_weights(rho, disp, act, pre_g, out_g, *refs):
    outs, (grad_in, grad_out) = refs[:8], refs[8:]
    for e in range(2):
        grad_in[e] = tn(disp[e], pre_g[e]).astype(bf16)
        grad_out[e] = tn(act[e], out_g[e]).astype(bf16)
    for k in range(8):
        a = pl.multiple_of(rho[k] * TOK, TOK)
        b = pl.multiple_of(rho[k] * 64, 64)
        for e in range(2):
            outs[k][TOK * e : TOK * (e + 1), :] = grad_in[e, pl.ds(a, TOK), :]
            outs[k][256 + 64 * e : 320 + 64 * e, :] = grad_out[e, pl.ds(b, 64), :]


def added(*refs):
    n = len(refs) // 3
    for a, b, out in zip(refs[:n], refs[n : 2 * n], refs[2 * n :]):
        out[...] = (a[...].astype(f32) + b[...].astype(f32)).astype(bf16)


def from_experts(t0, t1, t2, t3, gates, hidden, cot, gain, w, wo, *refs):
    attn_grad, hidden_grad, branch, logit_low, gain_row = refs
    total = t0[...].astype(f32) + t1[...].astype(f32) + t2[...].astype(f32) + t3[...].astype(f32)
    lane = lanes((TOK, TOK))
    g = total[:, D : D + TOK]
    g = jnp.where(lane < 32, g + pltpu.roll(g, 96, 1), 0.0)
    gate = gates[...]
    picked = gate * (g - jnp.sum(gate * g, axis=-1, keepdims=True))
    low = picked.astype(bf16)
    logit_low[...] = low
    grad = total[:, 0:D] + nt(low, w[:, 256:384])
    h = hidden[...]
    r = lax.rsqrt(jnp.mean(h * h, axis=-1, keepdims=True) + EPS)
    gain_row[...] = jnp.sum(grad * h * r, axis=0, keepdims=True)
    scaled = grad * gain[1:2, :]
    dot = jnp.mean(h * scaled, axis=-1, keepdims=True)
    out = cot[...].astype(f32) + r * scaled - h * (r * r * r * dot)
    hidden_grad[...] = out
    b = out.astype(bf16)
    branch[...] = b
    ag = nt(b, wo[...]).astype(bf16)
    for j in range(8):
        attn_grad[j] = ag[:, TOK * j : TOK * (j + 1)]


def dense_grads(sigma, low, branch, payload, logit_low, gain_row, *refs):
    outs, (whole,) = refs[:16], refs[16:]
    whole[:, 0:D] = tn(low[...], branch[...]).astype(bf16)
    router = tn(payload[:, 0:D], logit_low[...])
    lane = lanes((TOK, TOK))
    for j in range(8):
        at = slice(TOK * j, TOK * (j + 1))
        col = jnp.transpose(jnp.broadcast_to(gain_row[:, at], (TOK, TOK)))
        whole[at, D : D + TOK] = jnp.where(lane == 32, col, router[at, :]).astype(bf16)
    for k in range(16):
        outs[k][...] = whole[pl.ds(pl.multiple_of(sigma[k] * 64, 64), 64), :]


def weight_grad(norm, low, out):
    out[...] = tn(norm[...], low[...]).astype(bf16)


def to_input(low, wq, wkv, x, gain, hidden_grad, out):
    q = jnp.concatenate([low[r, :, 0:128] for r in range(8)], axis=1)
    kv = jnp.concatenate([low[r, :, 128:256] for r in range(8)], axis=1)
    grad = nt(q, wq[...]) + nt(kv, wkv[...])
    h = x[...].astype(f32)
    r = lax.rsqrt(jnp.mean(h * h, axis=-1, keepdims=True) + EPS)
    scaled = grad * gain[0:1, :]
    dot = jnp.mean(h * scaled, axis=-1, keepdims=True)
    out[...] = hidden_grad[...] + r * scaled - h * (r * r * r * dot)


def finished(rho, wq, wkv, gain, *refs):
    parts = refs[:8]
    out_q, out_kv, out_o, out_small, out_gain, pairs = refs[8:]
    total = jnp.zeros((64, D + TOK), f32)
    for k in range(8):
        total = total + parts[k][:, 0 : D + TOK].astype(f32)
        at = rho[k]
        out_q[:, pl.ds(pl.multiple_of(at * TOK, TOK), TOK)] = parts[k][
            :, D + TOK : D + 2 * TOK
        ].astype(f32)
        pairs[at] = parts[k][:, D + 2 * TOK : D + 3 * TOK].astype(f32)
    out_o[...] = total[:, 0:D]
    out_small[...] = total[:, D:]
    first = lanes((64, TOK)) < HD
    for j in range(4):
        a, b = pairs[2 * j], pairs[2 * j + 1]
        out_kv[:, TOK * j : TOK * (j + 1)] = jnp.where(first, a, pltpu.roll(b, HD, 1))
        out_kv[:, 512 + TOK * j : 512 + TOK * (j + 1)] = jnp.where(first, pltpu.roll(a, HD, 1), b)
    both = out_q[...] * wq[...].astype(f32) + out_kv[...] * wkv[...].astype(f32)
    out_gain[...] = jnp.sum(both, axis=-1, keepdims=True) / gain[...].astype(f32)


def body(
    layer_input,
    cotangent,
    gain_attn,
    w_query,
    w_keyval,
    w_output,
    gain_moe,
    w_router,
    w_in,
    w_out,
    routes,
    priority,
    block_ids,
):
    x = layer_input.reshape(TOK, D)
    cot = cotangent.reshape(TOK, D)
    route_rows = routes.reshape(TOK, TOPK)
    order_row = priority.reshape(1, TOK)
    marks = block_ids.reshape(1, TOK)
    rep = lax.axis_index(REP)
    shard = lax.axis_index(SHARD)
    core = lax.axis_index("c")
    rho = jnp.stack(owners("xl", "z", core)).astype(jnp.int32)
    sigma = jnp.stack(
        [2 * o + core for o in owners("xh", "y", core)]
        + [2 * o + 1 - core for o in owners("xh", "y", 1 - core)]
    ).astype(jnp.int32)
    who = shard.astype(jnp.int32).reshape(1)

    small = jnp.concatenate(
        [
            lax.dynamic_slice(w_query, (0, rep * 128), (64, 128)),
            lax.dynamic_slice(w_keyval, (0, rep * 64), (64, 64)),
            lax.dynamic_slice(w_keyval, (0, 512 + rep * 64), (64, 64)),
            w_router,
            gain_attn[:, None],
            gain_moe[:, None],
            jnp.zeros((64, 94), bf16),
        ],
        axis=1,
    )
    small = lax.all_gather(small, SHARD, axis=0, tiled=True)
    xs = spread(x, "xl", "z")
    seq_marks = spread(marks, "xl", "z")
    early = spread(jnp.concatenate([w_output, cot], axis=0), "xh", "y")
    early = early + [cross(e, "c") for e in early]
    wkv_pairs = w_keyval.reshape(64, 2, 8, 64).transpose(0, 2, 1, 3).reshape(64, D)
    wq_full = lax.all_gather(w_query, SHARD, axis=0, tiled=True)
    wkv_full = lax.all_gather(wkv_pairs, SHARD, axis=0, tiled=True)

    cos, sin = (jnp.asarray(t) for t in rope_tables())
    norm, q, kv, attn, low_cols, lse, gain = call(
        attend,
        "attend",
        [rho],
        [small, cos, sin, *xs, *seq_marks],
        [
            struct((LEN, D), bf16),
            struct((LEN, 128), bf16),
            struct((LEN, 128), bf16),
            struct((LEN, 128), f32),
            struct((LEN, 128), bf16),
            struct((LEN, 128), f32),
            struct((8, D), f32),
        ],
        [pltpu.VMEM((8, TOK), f32)],
        flops=2 * LEN * D * 256 + 8 * LEN * LEN * 128,
    )
    attn_in = lax.all_to_all(low_cols.reshape(8, TOK, 128), REP, 0, 0, tiled=True)
    wo, low, hidden, payload, gates = call(
        to_experts,
        "to_experts",
        [sigma],
        [x, attn_in, route_rows, order_row, gain, small, *early],
        [
            struct((D, D), bf16),
            struct((TOK, D), bf16),
            struct((TOK, D), f32),
            struct((TOK, D + TOK), bf16),
            struct((TOK, TOK), f32),
        ],
        flops=2 * TOK * D * D,
    )
    tokens = spread(payload, "xh", "y")
    tokens = tokens + [cross(t, "c") for t in tokens]
    found = call(
        experts,
        "experts",
        [who],
        [w_in, w_out, *tokens, *early],
        [
            struct((2, SLOTS, D), bf16),
            struct((2, SLOTS, F), bf16),
            struct((2, SLOTS, 2 * F), bf16),
            struct((2, SLOTS, D), bf16),
            *[struct((TOK, D + TOK), bf16)] * 16,
            *[struct((TOK, D), bf16)] * 16,
        ],
        [
            pltpu.VMEM((256, TOK), f32),
            pltpu.VMEM((8, 4 * CAP, 256), bf16),
            pltpu.VMEM((2, SLOTS, D), bf16),
            pltpu.VMEM((2, SLOTS, 1), f32),
            pltpu.VMEM((2, SLOTS, D), bf16),
            pltpu.VMEM((2, SLOTS, D), bf16),
            pltpu.VMEM((2, SLOTS, TOK), bf16),
        ],
        flops=8 * SLOTS * D * 3 * F,
        vmem=60,
    )
    disp, act, pre_g, out_g = found[:4]
    own_s, other_s, own_r, other_r = (found[4 + 8 * n : 12 + 8 * n] for n in range(4))

    def summed(own, other, name):
        arrived = [cross(o, "c") for o in other]
        width = own[0].shape[1]
        out = call(added, name, [], [*own, *arrived], [struct((TOK, width), bf16)] * 8)
        return collect(out, "xh", "y")

    terms = summed(own_s, other_s, "slot_sums")
    parts = call(
        expert_weights,
        "expert_weights",
        [rho],
        [disp, act, pre_g, out_g],
        [struct((384, D), bf16)] * 8,
        [pltpu.VMEM((2, D, 2 * F), bf16), pltpu.VMEM((2, F, D), bf16)],
        flops=4 * SLOTS * D * 3 * F,
    )
    expert_terms = collect(parts, "xl", "z")
    attn_grad, hidden_grad, branch, logit_low, gain_row = call(
        from_experts,
        "from_experts",
        [],
        [*terms, gates, hidden, cot, gain, small, wo],
        [
            struct((8, TOK, 128), bf16),
            struct((TOK, D), f32),
            struct((TOK, D), bf16),
            struct((TOK, TOK), bf16),
            struct((1, D), f32),
        ],
        flops=2 * TOK * D * D,
    )
    attn_grad = lax.all_to_all(attn_grad, REP, 0, 0, tiled=True).reshape(LEN, 128)
    result_terms = summed(own_r, other_r, "result_sums")
    dense = call(
        dense_grads,
        "dense_grads",
        [sigma],
        [low, branch, payload, logit_low, gain_row],
        [struct((64, D + TOK), bf16)] * 16,
        [pltpu.VMEM((D, D + TOK), bf16)],
        flops=2 * TOK * D * D,
    )
    dense_in = [cross(o, "c") for o in dense[8:]]
    dense = call(added, "dense_sums", [], [*dense[:8], *dense_in], [struct((64, D + TOK), bf16)] * 8)
    dense = collect(dense, "xh", "y")
    qkv_low = call(
        attend_back,
        "attend_back",
        [rho],
        [cos, sin, q, kv, attn, lse, attn_grad, *seq_marks],
        [struct((LEN, 256), bf16)],
        [pltpu.VMEM((8, TOK), f32), pltpu.VMEM((LEN, 128), f32), pltpu.VMEM((LEN, 128), f32)],
        flops=20 * LEN * LEN * 128,
    )[0]
    low_rows = lax.all_to_all(qkv_low.reshape(8, TOK, 256), REP, 0, 0, tiled=True)
    wgrad = call(
        weight_grad,
        "weight_grad",
        [],
        [norm, qkv_low],
        [struct((D, 256), bf16)],
        flops=2 * LEN * D * 256,
    )[0]
    wgrad = lax.all_to_all(wgrad.reshape(16, 64, 256), SHARD, 0, 0, tiled=True)
    wgrad = jnp.sum(wgrad.astype(f32), axis=0).astype(bf16)
    last = spread(jnp.concatenate([plus(*dense), wgrad], axis=1), "xl", "z")
    grad_input = call(
        to_input,
        "to_input",
        [],
        [low_rows, wq_full, wkv_full, x, gain, hidden_grad],
        [struct((TOK, D), f32)],
        flops=4 * TOK * D * D,
    )[0]
    grad_q, grad_kv, grad_o, grad_small, grad_gain = call(
        finished,
        "finished",
        [rho],
        [w_query, w_keyval, gain_attn.reshape(64, 1), *last],
        [
            struct((64, D), f32),
            struct((64, D), f32),
            struct((64, D), f32),
            struct((64, TOK), f32),
            struct((64, 1), f32),
        ],
        [pltpu.VMEM((8, 64, TOK), f32)],
    )
    result = hidden
    for t in result_terms:
        result = result + t.astype(f32)
    experts_sum = expert_terms[0].astype(f32)
    for t in expert_terms[1:]:
        experts_sum = experts_sum + t.astype(f32)
    return (
        result.astype(bf16).reshape(layer_input.shape),
        grad_input.reshape(layer_input.shape),
        grad_gain.reshape(64),
        grad_q,
        grad_kv,
        grad_o,
        grad_small[:, 32],
        grad_small[:, 0:32],
        experts_sum[0:256].reshape(2, TOK, D),
        experts_sum[256:384].reshape(2, 64, D),
    )


def solution(mesh):
    split = Mesh(mesh.devices.reshape(tuple(SIZES.values())), tuple(SIZES))
    tokens = P(SHARD, REP, None)
    weight = P(SHARD, None)
    return jax.shard_map(
        body,
        mesh=split,
        in_specs=(
            tokens,
            tokens,
            P(SHARD),
            weight,
            weight,
            weight,
            P(SHARD),
            weight,
            P(SHARD, None, None),
            P(SHARD, None, None),
            tokens,
            tokens,
            P(SHARD, REP),
        ),
        out_specs=(
            tokens,
            tokens,
            P(SHARD),
            weight,
            weight,
            weight,
            P(SHARD),
            weight,
            tokens,
            tokens,
        ),
        check_vma=False,
    )
```

```python
import itertools

import jax
import jax.numpy as jnp
import numpy as np
from jax import lax
from jax.experimental import pallas as pl
from jax.experimental.pallas import tpu as pltpu
from jax.sharding import Mesh
from jax.sharding import PartitionSpec as P

HEADS = 16
KV = 8
HD = 64
EXPERTS = 32
TOPK = 8
CAP = 40
TOK = 128
D = 1024
F = 512
LEN = 1024
EPS = 1e-06
SHARD = ("xh", "y", "c")
REP = ("xl", "z")
SIZES = {"xh": 2, "y": 4, "c": 2, "xl": 2, "z": 4}
bf16 = jnp.bfloat16
f32 = jnp.float32

VM = pl.BlockSpec(memory_space=pltpu.VMEM)
SM = pl.BlockSpec(memory_space=pltpu.SMEM)
ANY = pl.BlockSpec(memory_space=pl.ANY)


def moved(x, axes, to):
    sizes = [SIZES[a] for a in axes]
    pairs = []
    for here in itertools.product(*[range(s) for s in sizes]):
        there = to(*here)
        a = b = 0
        for s, i, j in zip(sizes, here, there):
            a, b = a * s + i, b * s + j % s
        pairs.append((a, b))
    return lax.ppermute(x, axes, pairs)


def ring(x, axis, sign):
    if axis == "y":
        return moved(x, ("y", "c"), lambda y, c: (y + sign * (1 - 2 * c), c))
    return moved(x, ("c", "z"), lambda c, z: (c, z + sign * (1 - 2 * c)))


def cross(x, axis):
    return moved(x, (axis,), lambda i: (1 - i,))


def spread(x, pair, axis):
    across = cross(x, pair)
    a = ring(x, axis, 1)
    b = ring(x, axis, -1)
    xa = ring(across, axis, 1)
    xb = ring(across, axis, -1)
    a2 = ring(a, axis, 1)
    xa2 = ring(xa, axis, 1)
    return [x, a, b, a2, across, xa, xb, xa2]


def owners(pair, ring_at, core):
    way = 1 - 2 * core
    return [p * 4 + (ring_at + s * way) % 4 for p in (pair, 1 - pair) for s in (0, -1, 1, -2)]


def places():
    table = []
    for xh, y, c, xl, z in itertools.product(*[range(s) for s in SIZES.values()]):
        mine = [2 * o + c for o in owners(xh, y, c)]
        other = [2 * o + 1 - c for o in owners(xh, y, 1 - c)]
        table.append([*owners(xl, z, c), *mine, *other, (xh * 4 + y) * 2 + c, xl * 4 + z, *[0] * 6])
    return np.array(table, np.int32)


def plus(*terms):
    total = terms[0].astype(f32)
    for t in terms[1:]:
        total = total + t.astype(f32)
    return total.astype(bf16)


def collect(own, a, b, a2, pair, axis):
    from_b = ring(b, axis, 1)
    step = plus(a, ring(a2, axis, -1))
    from_a = ring(step, axis, -1)
    return [own, from_b, from_a, cross(plus(own[1], from_b[1], from_a[1]), pair)], step


def collect_fast(near, far, pair, axis):
    r2 = ring(far[3], axis, -1)
    rb = ring(far[2], axis, 1)
    s2 = ring(near[3], axis, -1)
    sb = ring(near[2], axis, 1)
    ra = ring(plus(far[1], r2), axis, -1)
    sa = ring(plus(near[1], s2), axis, -1)
    return [near[0], sb, sa, cross(plus(far[0], rb, ra), pair)]


def nn(a, b):
    return jnp.dot(a, b, preferred_element_type=f32)


def nt(a, b):
    return lax.dot_general(a, b, (((1,), (1,)), ((), ())), preferred_element_type=f32)


def tn(a, b):
    return lax.dot_general(a, b, (((0,), (0,)), ((), ())), preferred_element_type=f32)


def lanes(shape):
    return lax.broadcasted_iota(jnp.int32, shape, len(shape) - 1)


def rows(shape):
    return lax.broadcasted_iota(jnp.int32, shape, 0)


def call(
    kernel, name, scalars, arrays, outs, scratch=(), us=3, vmem=56, far=0, far_outs=0, after=()
):
    given = len(scalars) + len(arrays)

    def run(*refs):
        kernel(*refs[:given], *refs[given + len(after) :])

    return pl.pallas_call(
        run,
        name=name,
        out_shape=outs,
        in_specs=[SM] * len(scalars) + [VM] * (len(arrays) - far) + [ANY] * (far + len(after)),
        out_specs=[ANY] * far_outs + [VM] * (len(outs) - far_outs),
        scratch_shapes=list(scratch),
        compiler_params=pltpu.CompilerParams(vmem_limit_bytes=vmem << 20),
        cost_estimate=pl.CostEstimate(
            flops=0, bytes_accessed=us * 3690000, transcendentals=0
        ),
    )(*scalars, *arrays, *after)


def struct(shape, dtype):
    return jax.ShapeDtypeStruct(shape, dtype)


def rope_tables():
    half = HD // 2
    frequency = np.power(10000.0, np.arange(half) * (-2.0 / HD))
    angles = np.arange(LEN)[:, None] * frequency[None, :]
    cosine, sine = np.cos(angles), np.sin(angles)
    return (
        np.concatenate([cosine] * 4, axis=1).astype(np.float32),
        np.concatenate([-sine, sine, -sine, sine], axis=1).astype(np.float32),
    )


def halves_swapped(x):
    first = lanes(x.shape) % HD < HD // 2
    return jnp.where(first, pltpu.roll(x, 96, 1), pltpu.roll(x, 32, 1))


def block_column(marks, j):
    return jnp.transpose(jnp.broadcast_to(marks[j : j + 1, :], (TOK, TOK)))[:, 0:1]


QB = 256


def visible_of(marks, i):
    reach = min(LEN, QB * (i + 2))
    row = jnp.concatenate([marks[j : j + 1, :] for j in range(reach // TOK)], axis=1)
    col = jnp.concatenate(
        [block_column(marks, j) for j in range(QB // TOK * i, QB // TOK * (i + 1))], axis=0
    )
    return reach, row <= col


def prepare(where, x, marks, wq, wkv, router, gain_a, gain_m, payload, small):
    payload[0:TOK, :] = x[...]
    payload[TOK : TOK + 16, :] = jnp.zeros((16, D), bf16)
    ids = jnp.where(rows((16, TOK)) == 0, marks[...].astype(f32), 0.0)
    payload[TOK : TOK + 16, 0:TOK] = ids.astype(bf16)
    rep = where[25]
    mine = pl.ds(pl.multiple_of(rep * 128, 128), 128)
    pair = lax.div(rep, 2)
    odd = jnp.full((64, 128), lax.rem(rep, 2)) == 1
    key = wkv[:, pl.ds(pl.multiple_of(pair * 128, 128), 128)].astype(f32)
    value = wkv[:, pl.ds(pl.multiple_of(512 + pair * 128, 128), 128)].astype(f32)
    key = jnp.where(odd, pltpu.roll(key, HD, 1), key)
    value = jnp.where(odd, value, pltpu.roll(value, HD, 1))
    kv = jnp.where(lanes((64, 128)) < HD, key, value).astype(bf16)
    diagonal = rows((64, 64)) == lanes((64, 64))
    gains = []
    for gain in (gain_a, gain_m):
        row = jnp.broadcast_to(gain[...].astype(f32), (64, 64))
        gains.append(jnp.sum(jnp.where(diagonal, row, 0.0), axis=1, keepdims=True))
    lane = lanes((64, 128))
    extra = jnp.where(lane == 32, gains[0], jnp.where(lane == 33, gains[1], 0.0)).astype(bf16)
    q = wq[:, mine]
    for n in range(16):
        small[n, :, 0:128] = q
        small[n, :, 128:256] = kv
        small[n, :, 256:384] = extra
        small[n, :, 256:288] = router[...]


def attend(rho, w, cos, sin, *refs):
    xs = refs[:8]
    norm, q_out, kv_out, attn_out, low_out, lse_out, gain_out, marks_out = refs[8:16]
    for j in range(8):
        part = jnp.transpose(w[TOK * j : TOK * (j + 1), 256:384].astype(f32))
        gain_out[0:8, TOK * j : TOK * (j + 1)] = part[32:40, :]
    gain = gain_out[0:1, :]
    for k in range(8):
        at = rho[k]
        marks_out[pl.ds(at, 1), :] = xs[k][TOK : TOK + 16, 0:TOK].astype(f32)[0:1]
        x = xs[k][0:TOK, :].astype(f32)
        inv = lax.rsqrt(jnp.mean(x * x, axis=-1, keepdims=True) + EPS)
        norm[pl.ds(pl.multiple_of(at * TOK, TOK), TOK), :] = (x * inv * gain).astype(bf16)
    marks = marks_out[...]
    pre = nn(norm[...], w[:, 0:256])
    c, s = cos[...], sin[...]
    q = pre[:, 0:128]
    q_out[...] = ((q * c + halves_swapped(q) * s) * (HD**-0.5)).astype(bf16)
    kv = pre[:, 128:256]
    is_key = lanes(kv.shape) < HD
    kv_out[...] = jnp.where(is_key, kv * c + halves_swapped(kv) * s, kv).astype(bf16)
    kvf = kv_out[...].astype(f32)
    turned = pltpu.roll(kvf, HD, 1)
    keys = jnp.where(is_key, kvf, turned).astype(bf16)
    values = jnp.where(is_key, turned, kvf).astype(bf16)
    for i in range(LEN // QB):
        reach, visible = visible_of(marks, i)
        at = slice(QB * i, QB * (i + 1))
        qi = q_out[at, :]
        first = lanes(qi.shape) < HD
        mixed, logs = [], []
        for h in range(2):
            qh = jnp.where(first == (h == 0), qi, jnp.zeros_like(qi))
            scores = jnp.where(visible, nt(qh, keys[:reach]), -1e30)
            top = jnp.max(scores, axis=-1, keepdims=True)
            e = jnp.exp(scores - top)
            total = jnp.sum(e, axis=-1, keepdims=True)
            mixed.append(nn(e.astype(bf16), values[:reach]) / total)
            logs.append(top + jnp.log(total))
        attn = jnp.where(first, mixed[0], mixed[1])
        attn_out[at, :] = attn
        low_out[at, :] = attn.astype(bf16)
        lse_out[at, :] = jnp.where(first, logs[0], logs[1])


def attend_back(where, cos, sin, q, kv, attn, lse, grad, marks_in, w, norm, wgrad, *refs):
    pairs, (out, dk, dv) = refs[:4], refs[4:]
    marks = marks_in[...]
    kvf = kv[...].astype(f32)
    is_key = lanes(kvf.shape) < HD
    turned = pltpu.roll(kvf, HD, 1)
    keys = jnp.where(is_key, kvf, turned).astype(bf16)
    values = jnp.where(is_key, turned, kvf).astype(bf16)
    dk[...] = jnp.zeros_like(dk)
    dv[...] = jnp.zeros_like(dv)
    for i in range(LEN // QB):
        reach, visible = visible_of(marks, i)
        at = slice(QB * i, QB * (i + 1))
        qi, gi = q[at, :], grad[at, :]
        first = lanes(qi.shape) < HD
        part = gi.astype(f32) * attn[at, :]
        dq = []
        for h in range(2):
            mine = first == (h == 0)
            qh = jnp.where(mine, qi, jnp.zeros_like(qi))
            gh = jnp.where(mine, gi, jnp.zeros_like(gi))
            delta = jnp.sum(jnp.where(mine, part, 0.0), axis=-1, keepdims=True)
            scores = nt(qh, keys[:reach])
            log = lse[at, HD * h : HD * h + 1]
            weights = jnp.where(visible, jnp.exp(scores - log), 0.0)
            low = (weights * (nt(gh, values[:reach]) - delta)).astype(bf16)
            dq.append(nn(low, keys[:reach]))
            dk[:reach, :] += tn(low, qh)
            dv[:reach, :] += tn(weights.astype(bf16), gh)
        g = jnp.where(first, dq[0], dq[1]) * (HD**-0.5)
        c, s = cos[at, :], sin[at, :]
        out[at, 0:128] = (g * c - halves_swapped(g) * s).astype(bf16)
    key = dk[...]
    key = key + pltpu.roll(key, HD, 1)
    val = dv[...]
    val = val + pltpu.roll(val, HD, 1)
    key = key * cos[...] - halves_swapped(key) * sin[...]
    out[:, 128:256] = jnp.where(is_key, key, val).astype(bf16)
    wgrad[...] = tn(norm[...], out[...]).astype(bf16)
    for k in range(8):
        at = pl.multiple_of(where[k] * TOK, TOK)
        pairs[k % 4][k // 4] = nt(out[pl.ds(at, TOK), :], w[:, 0:256]).astype(bf16)


def to_experts(
    x, attn, routes, priority, gain, w, early, wo, low, hidden, payload, gates_out, sems
):
    copies = []
    for s in range(16):
        to = wo.at[64 * s : 64 * (s + 1), :]
        copies.append(pltpu.make_async_copy(early.at[s, 0:64, :], to, sems.at[s]))
        copies[-1].start()
    for r in range(8):
        low[:, TOK * r : TOK * (r + 1)] = attn[r]
    for copy in copies:
        copy.wait()
    h = x[...].astype(f32) + nn(low[...], wo[...])
    hidden[...] = h
    inv = lax.rsqrt(jnp.mean(h * h, axis=-1, keepdims=True) + EPS)
    normed = (h * inv * gain[1:2, :]).astype(bf16)
    payload[:, 0:D] = normed
    logits = nn(normed, w[:, 256:384])
    lane = lanes((TOK, TOK))
    member = lane == routes[:, 0:1]
    for k in range(1, TOPK):
        member = member | (lane == routes[:, k : k + 1])
    order = jnp.broadcast_to(priority[...], (TOK, TOK)).astype(f32)
    earlier = (order < jnp.transpose(order)).astype(f32).astype(bf16)
    before = nn(earlier, member.astype(f32).astype(bf16))
    kept = member & (before < CAP)
    top = jnp.max(jnp.where(member, logits, -1e30), axis=-1, keepdims=True)
    e = jnp.where(member, jnp.exp(jnp.where(member, logits - top, 0.0)), 0.0)
    gates = e / jnp.sum(e, axis=-1, keepdims=True)
    gates_out[...] = gates
    high = gates.astype(bf16).astype(f32)
    rank = jnp.where(kept, before, -1.0)
    meta = jnp.where(
        lane < 32,
        rank,
        jnp.where(lane < 64, pltpu.roll(high, 32, 1), pltpu.roll(gates - high, 64, 1)),
    )
    payload[:, D : D + TOK] = jnp.transpose(meta).astype(bf16)


SLOTS = 16 * CAP


def assignment(pair, xb, meta, first, gate_col, at):
    two = 2 * CAP
    side = rows((two, 256)) >= CAP
    place = (rows((two, 256)) - jnp.where(side, CAP, 0)).astype(f32)
    here = side == (lanes((two, 256)) >= TOK)
    chosen = []
    for n, k in enumerate(pair):
        meta[TOK * n : TOK * (n + 1), :] = xb[k, :, D : D + TOK].astype(f32)
    for e in range(2):
        def line(offset):
            return jnp.concatenate(
                [meta[pl.ds(TOK * n + offset + first + e, 1), :] for n in range(2)], axis=1
            )

        pick = jnp.where((line(0) == place) & here, 1.0, 0.0)
        gate_col[e, at, :] = jnp.sum(pick * (line(32) + line(64)), axis=-1, keepdims=True)
        chosen.append(pick.astype(bf16))
    return jnp.concatenate(chosen, axis=0)


def fetches(who, xs, xb, x_sem, early, cb, c_sem):
    x_in = [pltpu.make_async_copy(xs[k], xb.at[k], x_sem.at[k]) for k in range(16)]
    c_in = []
    for k in range(16):
        source = early.at[who[8 + k], 64:192, :]
        c_in.append(pltpu.make_async_copy(source, cb.at[k], c_sem.at[k]))
    return x_in, c_in


def experts(who, *refs):
    xs, (w_in_far, w_out_far, cot_far) = refs[:16], refs[16:19]
    sums_far, (parts, own_r, other_r), sums = refs[19:23], refs[23:26], refs[26:30]
    act_o, pre_g, outs, picks, disp, out_g = refs[30:36]
    w_in, w_out, xb, cb, meta, cot_rows, gate_col, back, gg = refs[36:45]
    x_sem, c_sem, w_sem, o_sem, r_sem, g_sem = refs[45:]
    first = who[24] * 2
    two = 2 * CAP
    x_in, c_in = fetches(who, xs, xb, x_sem, cot_far, cb, c_sem)
    w_copies = []
    for e in range(2):
        w_copies.append(pltpu.make_async_copy(w_in_far.at[e], w_in.at[e], w_sem.at[2 * e]))
        w_copies.append(pltpu.make_async_copy(w_out_far.at[e], w_out.at[e], w_sem.at[2 * e + 1]))
    for p in range(8):
        x_in[p].start()
        x_in[p + 8].start()
    w_copies[0].start()
    w_copies[1].start()
    for p in range(8):
        c_in[p].start()
        c_in[p + 8].start()
    w_copies[2].start()
    w_copies[3].start()
    leaving = []

    def leave(source, to, sem):
        leaving.append(pltpu.make_async_copy(source, to, sem))
        leaving[-1].start()

    for p in range(8):
        at = slice(two * p, two * (p + 1))
        pair = (p, p + 8)
        for k in pair:
            x_in[k].wait()
        pick = assignment(pair, xb, meta, first, gate_col, at)
        picks[p] = pick
        found = nn(pick, jnp.concatenate([xb[k, :, 0:D] for k in pair], axis=0)).astype(bf16)
        for e in range(2):
            disp[e, at, :] = found[two * e : two * (e + 1)]
    for e in range(2):
        w_copies[2 * e].wait()
        pre = nn(disp[e], w_in[e])
        gate, up = pre[:, 0:F], pre[:, F : 2 * F]
        sig = 1.0 / (1.0 + jnp.exp(-gate))
        silu = gate * sig
        act = (silu * up).astype(bf16)
        act_o[e] = act
        w_copies[2 * e + 1].wait()
        out = nn(act, w_out[e])
        if e == 0:
            for p in range(8):
                at = slice(two * p, two * (p + 1))
                c_in[p].wait()
                c_in[p + 8].wait()
                cot = nn(picks[p], jnp.concatenate([cb[p], cb[p + 8]], axis=0))
                for n in range(2):
                    part = cot[two * n : two * (n + 1)]
                    cot_rows[n, at, :] = part.astype(bf16)
                    out_g[n, at, :] = (gate_col[n, at, :] * part).astype(bf16)
        g = jnp.sum(out * cot_rows[e].astype(f32), axis=-1, keepdims=True)
        high = g.astype(bf16).astype(f32)
        lane = lanes((SLOTS, TOK))
        gg[e] = jnp.where(
            lane == first + e, high, jnp.where(lane == first + e + 32, g - high, 0.0)
        ).astype(bf16)
        outs[e] = (gate_col[e] * out).astype(bf16)
        act_grad = nt(out_g[e], w_out[e])
        d_up = act_grad * silu
        d_gate = act_grad * up * (sig * (1.0 + gate * (1.0 - sig)))
        pre_g[e, :, 0:F] = d_gate.astype(bf16)
        pre_g[e, :, F : 2 * F] = d_up.astype(bf16)
        back[e] = nt(pre_g[e], w_in[e]).astype(bf16)
    for half in (1, 0):
        for p in range(4 * half, 4 * half + 4):
            at = slice(two * p, two * (p + 1))
            slot = jnp.concatenate([back[0, at, :], back[1, at, :]], axis=0)
            grads = jnp.concatenate([gg[0, at, :], gg[1, at, :]], axis=0)
            for n in range(2):
                whole = sums[2 * half + n].at[p % 4]
                pick = picks[p, :, TOK * n : TOK * (n + 1)]
                whole[:, 0:D] = tn(pick, slot).astype(bf16)
                whole[:, D : D + TOK] = tn(pick, grads).astype(bf16)
        for n in (2 * half + 1, 2 * half):
            leave(sums[n], sums_far[n], o_sem.at[n])
    for p in range(8):
        at = slice(two * p, two * (p + 1))
        value = jnp.concatenate([outs[0, at, :], outs[1, at, :]], axis=0)
        for n, to in enumerate((own_r, other_r)):
            k = p + 8 * n
            cb[k] = tn(picks[p, :, TOK * n : TOK * (n + 1)], value).astype(bf16)
            leave(cb.at[k], to.at[p % 4, p // 4], r_sem.at[k])

    def send(grad, e, count, row):
        for k in range(8):
            to = parts.at[k, row : row + count, :]
            sem = g_sem.at[e, k + 8 * (count == 64)]
            leave(grad.at[e, count * k : count * (k + 1), :], to, sem)

    for e in range(2):
        w_in[e] = tn(disp[e], pre_g[e]).astype(bf16)
        send(w_in, e, TOK, TOK * e)
        w_out[e] = tn(act_o[e], out_g[e]).astype(bf16)
        send(w_out, e, 64, 256 + 64 * e)
    for copy in leaving:
        copy.wait()


def expert_grads(total, grad_in, grad_out):
    for e in range(2):
        grad_in[e] = total[TOK * e : TOK * (e + 1), :].astype(f32)
        grad_out[e] = total[256 + 64 * e : 320 + 64 * e, :].astype(f32)


def added(a, b, *outs):
    for n, out in enumerate(outs):
        out[...] = (a[n].astype(f32) + b[n].astype(f32)).astype(bf16)


def layer_result(hidden, t0, t1, t2, t3, result):
    total = t0[0].astype(f32) + t1[0].astype(f32) + t2[0].astype(f32) + t3[...].astype(f32)
    result[...] = (hidden[...] + total).astype(bf16)


def last_terms(wgrad, t0, t1, t2, t3, last):
    total = t0[0].astype(f32) + t1[0].astype(f32) + t2[0].astype(f32) + t3[...].astype(f32)
    last[:, 0 : D + TOK] = total.astype(bf16)
    last[:, D + TOK :] = sum(wgrad[n].astype(f32) for n in range(16)).astype(bf16)


def from_experts(where, t0, t1, t2, t3, gates, hidden, cot, gain, w, wo, attn_low, payload, *refs):
    attn_grad, hidden_grad, own, other, whole = refs
    total = t0[...].astype(f32) + t1[...].astype(f32) + t2[...].astype(f32) + t3[...].astype(f32)
    lane = lanes((TOK, TOK))
    g = total[:, D : D + TOK]
    g = jnp.where(lane < 32, g + pltpu.roll(g, 96, 1), 0.0)
    gate = gates[...]
    picked = gate * (g - jnp.sum(gate * g, axis=-1, keepdims=True))
    low = picked.astype(bf16)
    grad = total[:, 0:D] + nt(low, w[:, 256:384])
    h = hidden[...]
    r = lax.rsqrt(jnp.mean(h * h, axis=-1, keepdims=True) + EPS)
    gain_row = jnp.sum(grad * h * r, axis=0, keepdims=True)
    scaled = grad * gain[1:2, :]
    dot = jnp.mean(h * scaled, axis=-1, keepdims=True)
    out = cot[...].astype(f32) + r * scaled - h * (r * r * r * dot)
    hidden_grad[...] = out
    b = out.astype(bf16)
    ag = nt(b, wo[...]).astype(bf16)
    for j in range(8):
        attn_grad[j] = ag[:, TOK * j : TOK * (j + 1)]
    whole[:, 0:D] = tn(attn_low[...], b).astype(bf16)
    router = tn(payload[:, 0:D], low)
    for j in range(8):
        at = slice(TOK * j, TOK * (j + 1))
        col = jnp.transpose(jnp.broadcast_to(gain_row[:, at], (TOK, TOK)))
        whole[at, D : D + TOK] = jnp.where(lane == 32, col, router[at, :]).astype(bf16)
    for k in range(8):
        for n, to in enumerate((own, other)):
            at = pl.multiple_of(where[8 + k + 8 * n] * 64, 64)
            to[k % 4, k // 4] = whole[pl.ds(at, 64), :]


def to_input(x, gain, hidden_grad, t0, t1, t2, t3, out):
    grad = t0[0].astype(f32) + t1[0].astype(f32) + t2[0].astype(f32) + t3[...].astype(f32)
    h = x[...].astype(f32)
    r = lax.rsqrt(jnp.mean(h * h, axis=-1, keepdims=True) + EPS)
    scaled = grad * gain[0:1, :]
    dot = jnp.mean(h * scaled, axis=-1, keepdims=True)
    out[...] = hidden_grad[...] + r * scaled - h * (r * r * r * dot)


def column_as_row(column):
    return jnp.transpose(jnp.broadcast_to(column, (64, TOK)))[0:1, :]


def finished(rho, wq, wkv, gain, *refs):
    parts = refs[:8]
    out_q, out_kv, out_o, out_router, out_moe, out_gain, pairs = refs[8:]
    total = jnp.zeros((64, D + TOK), f32)
    for k in range(8):
        total = total + parts[k][:, 0 : D + TOK].astype(f32)
        at = rho[k]
        out_q[:, pl.ds(pl.multiple_of(at * TOK, TOK), TOK)] = parts[k][
            :, D + TOK : D + 2 * TOK
        ].astype(f32)
        pairs[at] = parts[k][:, D + 2 * TOK : D + 3 * TOK].astype(f32)
    out_o[...] = total[:, 0:D]
    out_router[...] = total[:, D : D + EXPERTS]
    out_moe[...] = column_as_row(total[:, D + EXPERTS : D + EXPERTS + 1])
    first = lanes((64, TOK)) < HD
    for j in range(4):
        a, b = pairs[2 * j], pairs[2 * j + 1]
        out_kv[:, TOK * j : TOK * (j + 1)] = jnp.where(first, a, pltpu.roll(b, HD, 1))
        out_kv[:, 512 + TOK * j : 512 + TOK * (j + 1)] = jnp.where(first, pltpu.roll(a, HD, 1), b)
    both = out_q[...] * wq[...].astype(f32) + out_kv[...] * wkv[...].astype(f32)
    out_gain[...] = column_as_row(jnp.sum(both, axis=-1, keepdims=True)) / gain[...].astype(f32)


def body(
    layer_input,
    cotangent,
    gain_attn,
    w_query,
    w_keyval,
    w_output,
    gain_moe,
    w_router,
    w_in,
    w_out,
    routes,
    priority,
    block_ids,
):
    x = layer_input.reshape(TOK, D)
    cot = cotangent.reshape(TOK, D)
    route_rows = routes.reshape(TOK, TOPK)
    order_row = priority.reshape(1, TOK)
    marks = block_ids.reshape(1, TOK)
    where = lax.dynamic_index_in_dim(
        jnp.asarray(places()), lax.axis_index(tuple(SIZES)), keepdims=False
    )

    payload, small = call(
        prepare,
        "prepare",
        [where],
        [
            x,
            block_ids.reshape(1, TOK),
            w_query,
            w_keyval,
            w_router,
            gain_attn.reshape(1, 64),
            gain_moe.reshape(1, 64),
        ],
        [struct((TOK + 16, D), bf16), struct((16, 64, 384), bf16)],
        us=2,
    )
    xs = spread(payload, "xl", "z")
    small = lax.all_to_all(small, SHARD, 0, 0, tiled=True).reshape(D, 384)
    early = lax.all_gather(jnp.concatenate([w_output, cot], axis=0), SHARD, axis=0)
    cos, sin = (jnp.asarray(t) for t in rope_tables())
    norm, q, kv, attn, low_cols, lse, gain, seq_marks = call(
        attend,
        "attend",
        [where],
        [small, cos, sin, *xs],
        [
            struct((LEN, D), bf16),
            struct((LEN, 128), bf16),
            struct((LEN, 128), bf16),
            struct((LEN, 128), f32),
            struct((LEN, 128), bf16),
            struct((LEN, 128), f32),
            struct((8, D), f32),
            struct((8, TOK), f32),
        ],
        us=10,
    )
    attn_in = lax.all_to_all(low_cols.reshape(8, TOK, 128), REP, 0, 0, tiled=True)
    wo, low, hidden, payload, gates = call(
        to_experts,
        "to_experts",
        [],
        [x, attn_in, route_rows, order_row, gain, small, early],
        [
            struct((D, D), bf16),
            struct((TOK, D), bf16),
            struct((TOK, D), f32),
            struct((TOK, D + TOK), bf16),
            struct((TOK, TOK), f32),
        ],
        [pltpu.SemaphoreType.DMA((16,))],
        far=1,
        us=5,
    )
    tokens = spread(payload, "xh", "y")
    tokens = tokens + [cross(t, "c") for t in tokens]
    sums = [struct((4, TOK, D + TOK), bf16)] * 4
    own_0, other_0, own_1, other_1, parts, own_r, other_r = call(
        experts,
        "experts",
        [where],
        [*tokens, w_in, w_out, early],
        [*sums, struct((8, 384, D), bf16), *[struct((4, 2, TOK, D), bf16)] * 2],
        [
            *[pltpu.VMEM(k.shape, k.dtype) for k in sums],
            pltpu.VMEM((2, SLOTS, F), bf16),
            pltpu.VMEM((2, SLOTS, 2 * F), bf16),
            pltpu.VMEM((2, SLOTS, D), bf16),
            pltpu.VMEM((8, 4 * CAP, 256), bf16),
            pltpu.VMEM((2, SLOTS, D), bf16),
            pltpu.VMEM((2, SLOTS, D), bf16),
            pltpu.VMEM((2, D, 2 * F), bf16),
            pltpu.VMEM((2, F, D), bf16),
            pltpu.VMEM((16, TOK, D + TOK), bf16),
            pltpu.VMEM((16, TOK, D), bf16),
            pltpu.VMEM((256, TOK), f32),
            pltpu.VMEM((2, SLOTS, D), bf16),
            pltpu.VMEM((2, SLOTS, 1), f32),
            pltpu.VMEM((2, SLOTS, D), bf16),
            pltpu.VMEM((2, SLOTS, TOK), bf16),
            pltpu.SemaphoreType.DMA((16,)),
            pltpu.SemaphoreType.DMA((16,)),
            pltpu.SemaphoreType.DMA((4,)),
            pltpu.SemaphoreType.DMA((4,)),
            pltpu.SemaphoreType.DMA((16,)),
            pltpu.SemaphoreType.DMA((2, 16)),
        ],
        us=27,
        vmem=60,
        far=19,
        far_outs=7,
    )
    part = [struct((TOK, D + TOK), bf16)] * 4
    far = call(added, "far_sums", [], [own_1, cross(other_1, "c")], part)
    near = call(added, "near_sums", [], [own_0, cross(other_0, "c")], part)
    slot_terms = collect_fast(near, far, "xh", "y")
    r_pairs = call(
        added, "result_sums", [], [own_r, cross(other_r, "c")], [struct((2, TOK, D), bf16)] * 4
    )
    r_terms, r_step = collect(*r_pairs, "xh", "y")
    expert_sum = lax.psum_scatter(parts.reshape(-1, D), REP, scatter_dimension=0, tiled=True)
    attn_grad, hidden_grad, dense_own, dense_other = call(
        from_experts,
        "from_experts",
        [where],
        [*slot_terms, gates, hidden, cot, gain, small, wo, low, payload],
        [
            struct((8, TOK, 128), bf16),
            struct((TOK, D), f32),
            *[struct((4, 2, 64, D + TOK), bf16)] * 2,
        ],
        [pltpu.VMEM((D, D + TOK), bf16)],
        after=[r_pairs[0]],
        us=6,
    )
    attn_grad = lax.all_to_all(attn_grad, REP, 0, 0, tiled=True).reshape(LEN, 128)
    wgrad, *norm_terms = call(
        attend_back,
        "attend_back",
        [where],
        [cos, sin, q, kv, attn, lse, attn_grad, seq_marks, small, norm],
        [struct((D, 256), bf16), *[struct((2, TOK, D), bf16)] * 4],
        [
            pltpu.VMEM((LEN, 256), bf16),
            pltpu.VMEM((LEN, 128), f32),
            pltpu.VMEM((LEN, 128), f32),
        ],
        us=13,
    )
    wgrad = lax.all_to_all(wgrad.reshape(16, 64, 256), SHARD, 0, 0, tiled=True)
    norm_terms, norm_step = collect(*norm_terms, "xl", "z")
    dense = call(
        added,
        "dense_sums",
        [],
        [dense_own, cross(dense_other, "c")],
        [struct((2, 64, D + TOK), bf16)] * 4,
    )
    dense_terms, _ = collect(*dense, "xh", "y")
    result = call(
        layer_result, "layer_result", [], [hidden, *r_terms], [struct((TOK, D), bf16)]
    )[0]
    grad_in, grad_out = call(
        expert_grads,
        "expert_grads",
        [],
        [expert_sum],
        [struct((2, TOK, D), f32), struct((2, 64, D), f32)],
    )
    last = call(
        last_terms,
        "last_terms",
        [],
        [wgrad, *dense_terms],
        [struct((64, D + 3 * TOK), bf16)],
        after=[norm_step, result, grad_in],
        us=2,
    )[0]
    last = spread(last, "xl", "z")
    grad_input = call(
        to_input,
        "to_input",
        [],
        [x, gain, hidden_grad, *norm_terms],
        [struct((TOK, D), f32)],
    )[0]
    grad_q, grad_kv, grad_o, grad_router, grad_moe, grad_gain = call(
        finished,
        "finished",
        [where],
        [w_query, w_keyval, gain_attn.reshape(1, 64), *last],
        [
            struct((64, D), f32),
            struct((64, D), f32),
            struct((64, D), f32),
            struct((64, EXPERTS), f32),
            struct((1, 64), f32),
            struct((1, 64), f32),
        ],
        [pltpu.VMEM((8, 64, TOK), f32)],
    )
    return (
        result.reshape(layer_input.shape),
        grad_input.reshape(layer_input.shape),
        grad_gain.reshape(64),
        grad_q,
        grad_kv,
        grad_o,
        grad_moe.reshape(64),
        grad_router,
        grad_in,
        grad_out,
    )


def solution(mesh):
    split = Mesh(mesh.devices.reshape(tuple(SIZES.values())), tuple(SIZES))
    tokens = P(SHARD, REP, None)
    weight = P(SHARD, None)
    return jax.shard_map(
        body,
        mesh=split,
        in_specs=(
            tokens,
            tokens,
            P(SHARD),
            weight,
            weight,
            weight,
            P(SHARD),
            weight,
            P(SHARD, None, None),
            P(SHARD, None, None),
            tokens,
            tokens,
            P(SHARD, REP),
        ),
        out_specs=(
            tokens,
            tokens,
            P(SHARD),
            weight,
            weight,
            weight,
            P(SHARD),
            weight,
            tokens,
            tokens,
        ),
        check_vma=False,
    )
```

```python
import itertools

import jax
import jax.numpy as jnp
import numpy as np
from jax import lax
from jax.experimental import pallas as pl
from jax.experimental.pallas import tpu as pltpu
from jax.sharding import Mesh
from jax.sharding import PartitionSpec as P

HEADS = 16
KV = 8
HD = 64
EXPERTS = 32
TOPK = 8
CAP = 40
TOK = 128
D = 1024
F = 512
LEN = 1024
EPS = 1e-06
SHARD = ("xh", "y", "c")
REP = ("xl", "z")
SIZES = {"xh": 2, "y": 4, "c": 2, "xl": 2, "z": 4}
bf16 = jnp.bfloat16
f32 = jnp.float32

VM = pl.BlockSpec(memory_space=pltpu.VMEM)
SM = pl.BlockSpec(memory_space=pltpu.SMEM)
ANY = pl.BlockSpec(memory_space=pl.ANY)


def moved(x, axes, to):
    sizes = [SIZES[a] for a in axes]
    pairs = []
    for here in itertools.product(*[range(s) for s in sizes]):
        there = to(*here)
        a = b = 0
        for s, i, j in zip(sizes, here, there):
            a, b = a * s + i, b * s + j % s
        pairs.append((a, b))
    return lax.ppermute(x, axes, pairs)


def ring(x, axis, sign):
    if axis == "y":
        return moved(x, ("y", "c"), lambda y, c: (y + sign * (1 - 2 * c), c))
    return moved(x, ("c", "z"), lambda c, z: (c, z + sign * (1 - 2 * c)))


def cross(x, axis):
    return moved(x, (axis,), lambda i: (1 - i,))


def spread(x, pair, axis):
    across = cross(x, pair)
    a = ring(x, axis, 1)
    b = ring(x, axis, -1)
    xa = ring(across, axis, 1)
    xb = ring(across, axis, -1)
    a2 = ring(a, axis, 1)
    xa2 = ring(xa, axis, 1)
    return [x, a, b, a2, across, xa, xb, xa2]


def owners(pair, ring_at, core):
    way = 1 - 2 * core
    return [p * 4 + (ring_at + s * way) % 4 for p in (pair, 1 - pair) for s in (0, -1, 1, -2)]


def places():
    table = []
    for xh, y, c, xl, z in itertools.product(*[range(s) for s in SIZES.values()]):
        mine = [2 * o + c for o in owners(xh, y, c)]
        other = [2 * o + 1 - c for o in owners(xh, y, 1 - c)]
        table.append([*owners(xl, z, c), *mine, *other, (xh * 4 + y) * 2 + c, xl * 4 + z, *[0] * 6])
    return np.array(table, np.int32)


def plus(*terms):
    total = terms[0].astype(f32)
    for t in terms[1:]:
        total = total + t.astype(f32)
    return total.astype(bf16)


def collect(own, a, b, a2, pair, axis):
    from_b = ring(b, axis, 1)
    step = plus(a, ring(a2, axis, -1))
    from_a = ring(step, axis, -1)
    return [own, from_b, from_a, cross(plus(own[1], from_b[1], from_a[1]), pair)], step


def collect_fast(near, far, pair, axis):
    r2 = ring(far[3], axis, -1)
    rb = ring(far[2], axis, 1)
    s2 = ring(near[3], axis, -1)
    sb = ring(near[2], axis, 1)
    ra = ring(plus(far[1], r2), axis, -1)
    sa = ring(plus(near[1], s2), axis, -1)
    return [near[0], sb, sa, cross(plus(far[0], rb, ra), pair)]


def nn(a, b):
    return jnp.dot(a, b, preferred_element_type=f32)


def nt(a, b):
    return lax.dot_general(a, b, (((1,), (1,)), ((), ())), preferred_element_type=f32)


def tn(a, b):
    return lax.dot_general(a, b, (((0,), (0,)), ((), ())), preferred_element_type=f32)


def lanes(shape):
    return lax.broadcasted_iota(jnp.int32, shape, len(shape) - 1)


def rows(shape):
    return lax.broadcasted_iota(jnp.int32, shape, 0)


def call(
    kernel, name, scalars, arrays, outs, scratch=(), us=3, vmem=56, far=0, far_outs=0, after=()
):
    given = len(scalars) + len(arrays)

    def run(*refs):
        kernel(*refs[:given], *refs[given + len(after) :])

    return pl.pallas_call(
        run,
        name=name,
        out_shape=outs,
        in_specs=[SM] * len(scalars) + [VM] * (len(arrays) - far) + [ANY] * (far + len(after)),
        out_specs=[ANY] * far_outs + [VM] * (len(outs) - far_outs),
        scratch_shapes=list(scratch),
        compiler_params=pltpu.CompilerParams(vmem_limit_bytes=vmem << 20),
        cost_estimate=pl.CostEstimate(
            flops=0, bytes_accessed=us * 3690000, transcendentals=0
        ),
    )(*scalars, *arrays, *after)


def struct(shape, dtype):
    return jax.ShapeDtypeStruct(shape, dtype)


def rope_tables():
    half = HD // 2
    frequency = np.power(10000.0, np.arange(half) * (-2.0 / HD))
    angles = np.arange(LEN)[:, None] * frequency[None, :]
    cosine, sine = np.cos(angles), np.sin(angles)
    return (
        np.concatenate([cosine] * 4, axis=1).astype(np.float32),
        np.concatenate([-sine, sine, -sine, sine], axis=1).astype(np.float32),
    )


def halves_swapped(x):
    first = lanes(x.shape) % HD < HD // 2
    return jnp.where(first, pltpu.roll(x, 96, 1), pltpu.roll(x, 32, 1))


def block_column(marks, j):
    return jnp.transpose(jnp.broadcast_to(marks[j : j + 1, :], (TOK, TOK)))[:, 0:1]


QB = 256


def visible_of(marks, i):
    reach = min(LEN, QB * (i + 2))
    row = jnp.concatenate([marks[j : j + 1, :] for j in range(reach // TOK)], axis=1)
    col = jnp.concatenate(
        [block_column(marks, j) for j in range(QB // TOK * i, QB // TOK * (i + 1))], axis=0
    )
    return reach, row <= col


def prepare(where, x, marks, wq, wkv, router, gain_a, gain_m, payload, small):
    payload[0:TOK, :] = x[...]
    payload[TOK : TOK + 16, :] = jnp.zeros((16, D), bf16)
    ids = jnp.where(rows((16, TOK)) == 0, marks[...].astype(f32), 0.0)
    payload[TOK : TOK + 16, 0:TOK] = ids.astype(bf16)
    rep = where[25]
    mine = pl.ds(pl.multiple_of(rep * 128, 128), 128)
    pair = lax.div(rep, 2)
    odd = jnp.full((64, 128), lax.rem(rep, 2)) == 1
    key = wkv[:, pl.ds(pl.multiple_of(pair * 128, 128), 128)].astype(f32)
    value = wkv[:, pl.ds(pl.multiple_of(512 + pair * 128, 128), 128)].astype(f32)
    key = jnp.where(odd, pltpu.roll(key, HD, 1), key)
    value = jnp.where(odd, value, pltpu.roll(value, HD, 1))
    kv = jnp.where(lanes((64, 128)) < HD, key, value).astype(bf16)
    diagonal = rows((64, 64)) == lanes((64, 64))
    gains = []
    for gain in (gain_a, gain_m):
        row = jnp.broadcast_to(gain[...].astype(f32), (64, 64))
        gains.append(jnp.sum(jnp.where(diagonal, row, 0.0), axis=1, keepdims=True))
    lane = lanes((64, 128))
    one = (rows((EXPERTS, 128)) == lanes((EXPERTS, 128))).astype(f32).astype(bf16)
    extra = tn(router[...], one)
    extra = jnp.where(lane == 32, gains[0], jnp.where(lane == 33, gains[1], extra)).astype(bf16)
    q = wq[:, mine]
    for n in range(16):
        small[n, :, 0:128] = q
        small[n, :, 128:256] = kv
        small[n, :, 256:384] = extra


def attend(rho, w, cos, sin, *refs):
    xs = refs[:8]
    norm, q_out, kv_out, attn_out, low_out, lse_out, gain_out, marks_out = refs[8:16]
    for j in range(8):
        part = jnp.transpose(w[TOK * j : TOK * (j + 1), 256:384].astype(f32))
        gain_out[0:8, TOK * j : TOK * (j + 1)] = part[32:40, :]
    gain = gain_out[0:1, :]
    for k in range(8):
        at = rho[k]
        marks_out[pl.ds(at, 1), :] = xs[k][TOK : TOK + 16, 0:TOK].astype(f32)[0:1]
        x = xs[k][0:TOK, :].astype(f32)
        inv = lax.rsqrt(jnp.mean(x * x, axis=-1, keepdims=True) + EPS)
        norm[pl.ds(pl.multiple_of(at * TOK, TOK), TOK), :] = (x * inv * gain).astype(bf16)
    marks = marks_out[...]
    pre = nn(norm[...], w[:, 0:256])
    c, s = cos[...], sin[...]
    q = pre[:, 0:128]
    q_out[...] = ((q * c + halves_swapped(q) * s) * (HD**-0.5)).astype(bf16)
    kv = pre[:, 128:256]
    is_key = lanes(kv.shape) < HD
    kv_out[...] = jnp.where(is_key, kv * c + halves_swapped(kv) * s, kv).astype(bf16)
    kvf = kv_out[...].astype(f32)
    turned = pltpu.roll(kvf, HD, 1)
    keys = jnp.where(is_key, kvf, turned).astype(bf16)
    values = jnp.where(is_key, turned, kvf).astype(bf16)
    for i in range(LEN // QB):
        reach, visible = visible_of(marks, i)
        at = slice(QB * i, QB * (i + 1))
        qi = q_out[at, :]
        first = lanes(qi.shape) < HD
        mixed, logs = [], []
        for h in range(2):
            qh = jnp.where(first == (h == 0), qi, jnp.zeros_like(qi))
            scores = jnp.where(visible, nt(qh, keys[:reach]), -1e30)
            top = jnp.max(scores, axis=-1, keepdims=True)
            e = jnp.exp(scores - top)
            total = jnp.sum(e, axis=-1, keepdims=True)
            mixed.append(nn(e.astype(bf16), values[:reach]) / total)
            logs.append(top + jnp.log(total))
        attn = jnp.where(first, mixed[0], mixed[1])
        attn_out[at, :] = attn
        low_out[at, :] = attn.astype(bf16)
        lse_out[at, :] = jnp.where(first, logs[0], logs[1])


def head_back(h, q, kv, attn, lse, grad, marks, dq, dk, dv):
    kvf = kv[...].astype(f32)
    is_key = lanes(kvf.shape) < HD
    turned = pltpu.roll(kvf, HD, 1)
    keys = jnp.where(is_key, kvf, turned).astype(bf16)
    values = jnp.where(is_key, turned, kvf).astype(bf16)
    for i in range(LEN // QB):
        reach, visible = visible_of(marks, i)
        at = slice(QB * i, QB * (i + 1))
        qi, gi = q[at, :], grad[at, :]
        mine = (lanes(qi.shape) < HD) == (h == 0)
        qh = jnp.where(mine, qi, jnp.zeros_like(qi))
        gh = jnp.where(mine, gi, jnp.zeros_like(gi))
        part = jnp.where(mine, gi.astype(f32) * attn[at, :], 0.0)
        delta = jnp.sum(part, axis=-1, keepdims=True)
        scores = nt(qh, keys[:reach])
        log = lse[at, HD * h : HD * h + 1]
        weights = jnp.where(visible, jnp.exp(scores - log), 0.0)
        low = (weights * (nt(gh, values[:reach]) - delta)).astype(bf16)
        dq[at, :] = jnp.where(mine, nn(low, keys[:reach]), dq[at, :])
        dk[:reach, :] += tn(low, qh)
        dv[:reach, :] += tn(weights.astype(bf16), gh)


def attend_back_0(q, kv, attn, lse, grad, marks_in, dq, dk, dv):
    dq[...] = jnp.zeros_like(dq)
    dk[...] = jnp.zeros_like(dk)
    dv[...] = jnp.zeros_like(dv)
    head_back(0, q, kv, attn, lse, grad, marks_in[...], dq, dk, dv)


def attend_back_1(where, cos, sin, q, kv, attn, lse, grad, marks_in, dq_in, dk_in, dv_in, w, norm, *refs):
    (wgrad, *pairs), (out, dq, dk, dv) = refs[:5], refs[5:]
    dq[...] = dq_in[...]
    dk[...] = dk_in[...]
    dv[...] = dv_in[...]
    head_back(1, q, kv, attn, lse, grad, marks_in[...], dq, dk, dv)
    c, s = cos[...], sin[...]
    g = dq[...] * (HD**-0.5)
    out[:, 0:128] = (g * c - halves_swapped(g) * s).astype(bf16)
    key = dk[...]
    key = key + pltpu.roll(key, HD, 1)
    val = dv[...]
    val = val + pltpu.roll(val, HD, 1)
    key = key * c - halves_swapped(key) * s
    out[:, 128:256] = jnp.where(lanes(key.shape) < HD, key, val).astype(bf16)
    wgrad[...] = tn(norm[...], out[...]).astype(bf16)
    for k in range(8):
        at = pl.multiple_of(where[k] * TOK, TOK)
        pairs[k % 4][k // 4] = nt(out[pl.ds(at, TOK), :], w[:, 0:256]).astype(bf16)


def to_experts(
    x, attn, routes, priority, gain, w, early, wo, low, hidden, payload, gates_out, sems
):
    copies = []
    for s in range(16):
        to = wo.at[64 * s : 64 * (s + 1), :]
        copies.append(pltpu.make_async_copy(early.at[s, 0:64, :], to, sems.at[s]))
        copies[-1].start()
    for r in range(8):
        low[:, TOK * r : TOK * (r + 1)] = attn[r]
    for copy in copies:
        copy.wait()
    h = x[...].astype(f32) + nn(low[...], wo[...])
    hidden[...] = h
    inv = lax.rsqrt(jnp.mean(h * h, axis=-1, keepdims=True) + EPS)
    normed = (h * inv * gain[1:2, :]).astype(bf16)
    payload[:, 0:D] = normed
    logits = nn(normed, w[:, 256:384])
    lane = lanes((TOK, TOK))
    member = lane == routes[:, 0:1]
    for k in range(1, TOPK):
        member = member | (lane == routes[:, k : k + 1])
    order = jnp.broadcast_to(priority[...], (TOK, TOK)).astype(f32)
    earlier = (order < jnp.transpose(order)).astype(f32).astype(bf16)
    before = nn(earlier, member.astype(f32).astype(bf16))
    kept = member & (before < CAP)
    top = jnp.max(jnp.where(member, logits, -1e30), axis=-1, keepdims=True)
    e = jnp.where(member, jnp.exp(jnp.where(member, logits - top, 0.0)), 0.0)
    gates = e / jnp.sum(e, axis=-1, keepdims=True)
    gates_out[...] = gates
    high = gates.astype(bf16).astype(f32)
    rank = jnp.where(kept, before, -1.0)
    meta = jnp.where(
        lane < 32,
        rank,
        jnp.where(lane < 64, pltpu.roll(high, 32, 1), pltpu.roll(gates - high, 64, 1)),
    )
    payload[:, D : D + TOK] = jnp.transpose(meta).astype(bf16)


SLOTS = 16 * CAP


def assignment(pair, xb, meta, first, gate_col, at):
    two = 2 * CAP
    side = rows((two, 256)) >= CAP
    place = (rows((two, 256)) - jnp.where(side, CAP, 0)).astype(f32)
    here = side == (lanes((two, 256)) >= TOK)
    chosen = []
    for n, k in enumerate(pair):
        meta[TOK * n : TOK * (n + 1), :] = xb[k, :, D : D + TOK].astype(f32)
    for e in range(2):
        def line(offset):
            return jnp.concatenate(
                [meta[pl.ds(TOK * n + offset + first + e, 1), :] for n in range(2)], axis=1
            )

        pick = jnp.where((line(0) == place) & here, 1.0, 0.0)
        gate_col[e, at, :] = jnp.sum(pick * (line(32) + line(64)), axis=-1, keepdims=True)
        chosen.append(pick.astype(bf16))
    return jnp.concatenate(chosen, axis=0)


def fetches(who, xs, xb, x_sem, early, cb, c_sem):
    x_in = [pltpu.make_async_copy(xs[k], xb.at[k], x_sem.at[k]) for k in range(16)]
    c_in = []
    for k in range(16):
        source = early.at[who[8 + k], 64:192, :]
        c_in.append(pltpu.make_async_copy(source, cb.at[k], c_sem.at[k]))
    return x_in, c_in


def experts(who, *refs):
    xs, (w_in_far, w_out_far, cot_far) = refs[:16], refs[16:19]
    sums_far, (parts, own_r, other_r), sums = refs[19:23], refs[23:26], refs[26:30]
    act_o, pre_g, outs, picks, disp, out_g = refs[30:36]
    w_in, w_out, xb, cb, meta, cot_rows, gate_col, back, gg = refs[36:45]
    x_sem, c_sem, w_sem, o_sem, r_sem, g_sem = refs[45:]
    first = who[24] * 2
    two = 2 * CAP
    x_in, c_in = fetches(who, xs, xb, x_sem, cot_far, cb, c_sem)
    w_copies = []
    for e in range(2):
        w_copies.append(pltpu.make_async_copy(w_in_far.at[e], w_in.at[e], w_sem.at[2 * e]))
        w_copies.append(pltpu.make_async_copy(w_out_far.at[e], w_out.at[e], w_sem.at[2 * e + 1]))
    for p in range(8):
        x_in[p].start()
        x_in[p + 8].start()
    w_copies[0].start()
    w_copies[1].start()
    for p in range(8):
        c_in[p].start()
        c_in[p + 8].start()
    w_copies[2].start()
    w_copies[3].start()
    leaving = []

    def leave(source, to, sem):
        leaving.append(pltpu.make_async_copy(source, to, sem))
        leaving[-1].start()

    for p in range(8):
        at = slice(two * p, two * (p + 1))
        pair = (p, p + 8)
        for k in pair:
            x_in[k].wait()
        pick = assignment(pair, xb, meta, first, gate_col, at)
        picks[p] = pick
        found = nn(pick, jnp.concatenate([xb[k, :, 0:D] for k in pair], axis=0)).astype(bf16)
        for e in range(2):
            disp[e, at, :] = found[two * e : two * (e + 1)]
    for e in range(2):
        w_copies[2 * e].wait()
        pre = nn(disp[e], w_in[e])
        gate, up = pre[:, 0:F], pre[:, F : 2 * F]
        sig = 1.0 / (1.0 + jnp.exp(-gate))
        silu = gate * sig
        act = (silu * up).astype(bf16)
        act_o[e] = act
        w_copies[2 * e + 1].wait()
        out = nn(act, w_out[e])
        if e == 0:
            for p in range(8):
                at = slice(two * p, two * (p + 1))
                c_in[p].wait()
                c_in[p + 8].wait()
                cot = nn(picks[p], jnp.concatenate([cb[p], cb[p + 8]], axis=0))
                for n in range(2):
                    part = cot[two * n : two * (n + 1)]
                    cot_rows[n, at, :] = part.astype(bf16)
                    out_g[n, at, :] = (gate_col[n, at, :] * part).astype(bf16)
        g = jnp.sum(out * cot_rows[e].astype(f32), axis=-1, keepdims=True)
        high = g.astype(bf16).astype(f32)
        lane = lanes((SLOTS, TOK))
        gg[e] = jnp.where(
            lane == first + e, high, jnp.where(lane == first + e + 32, g - high, 0.0)
        ).astype(bf16)
        outs[e] = (gate_col[e] * out).astype(bf16)
        act_grad = nt(out_g[e], w_out[e])
        d_up = act_grad * silu
        d_gate = act_grad * up * (sig * (1.0 + gate * (1.0 - sig)))
        pre_g[e, :, 0:F] = d_gate.astype(bf16)
        pre_g[e, :, F : 2 * F] = d_up.astype(bf16)
        back[e] = nt(pre_g[e], w_in[e]).astype(bf16)
    for half in (1, 0):
        for p in range(4 * half, 4 * half + 4):
            at = slice(two * p, two * (p + 1))
            slot = jnp.concatenate([back[0, at, :], back[1, at, :]], axis=0)
            grads = jnp.concatenate([gg[0, at, :], gg[1, at, :]], axis=0)
            for n in range(2):
                whole = sums[2 * half + n].at[p % 4]
                pick = picks[p, :, TOK * n : TOK * (n + 1)]
                whole[:, 0:D] = tn(pick, slot).astype(bf16)
                whole[:, D : D + TOK] = tn(pick, grads).astype(bf16)
        for n in (2 * half + 1, 2 * half):
            leave(sums[n], sums_far[n], o_sem.at[n])
    for p in range(8):
        at = slice(two * p, two * (p + 1))
        value = jnp.concatenate([outs[0, at, :], outs[1, at, :]], axis=0)
        for n, to in enumerate((own_r, other_r)):
            k = p + 8 * n
            cb[k] = tn(picks[p, :, TOK * n : TOK * (n + 1)], value).astype(bf16)
            leave(cb.at[k], to.at[p % 4, p // 4], r_sem.at[k])

    def send(grad, e, count, row):
        for k in range(8):
            to = parts.at[k, row : row + count, :]
            sem = g_sem.at[e, k + 8 * (count == 64)]
            leave(grad.at[e, count * k : count * (k + 1), :], to, sem)

    for e in range(2):
        w_in[e] = tn(disp[e], pre_g[e]).astype(bf16)
        send(w_in, e, TOK, TOK * e)
        w_out[e] = tn(act_o[e], out_g[e]).astype(bf16)
        send(w_out, e, 64, 256 + 64 * e)
    for copy in leaving:
        copy.wait()


def expert_grads(total, grad_in, grad_out):
    for e in range(2):
        grad_in[e] = total[TOK * e : TOK * (e + 1), :].astype(f32)
        grad_out[e] = total[256 + 64 * e : 320 + 64 * e, :].astype(f32)


def added(a, b, name, us=2):
    count = a.shape[0]

    def kernel(a_ref, b_ref, *outs):
        for n, out in enumerate(outs):

            @pl.when(pl.program_id(0) == n)
            def _(out=out):
                out[...] = (a_ref[0].astype(f32) + b_ref[0].astype(f32)).astype(bf16)

    zeros = (0,) * (a.ndim - 1)
    block = pl.BlockSpec((1, *a.shape[1:]), lambda i: (i, *zeros))
    return pl.pallas_call(
        kernel,
        name=name,
        out_shape=[struct(a.shape[1:], bf16)] * count,
        grid=(count,),
        in_specs=[block, block],
        out_specs=[pl.BlockSpec(a.shape[1:], lambda i: zeros)] * count,
        compiler_params=pltpu.CompilerParams(vmem_limit_bytes=32 << 20),
        cost_estimate=pl.CostEstimate(
            flops=0, bytes_accessed=us * 3690000, transcendentals=0
        ),
    )(a, b)


def layer_result(hidden, t0, t1, t2, t3, result):
    total = t0[0].astype(f32) + t1[0].astype(f32) + t2[0].astype(f32) + t3[...].astype(f32)
    result[...] = (hidden[...] + total).astype(bf16)


def last_terms(wgrad, t0, t1, t2, t3, last):
    total = t0[0].astype(f32) + t1[0].astype(f32) + t2[0].astype(f32) + t3[...].astype(f32)
    last[:, 0 : D + TOK] = total.astype(bf16)
    last[:, D + TOK :] = sum(wgrad[n].astype(f32) for n in range(16)).astype(bf16)


def from_experts(where, t0, t1, t2, t3, gates, hidden, cot, gain, w, wo, attn_low, payload, *refs):
    attn_grad, hidden_grad, own, other, whole = refs
    total = t0[...].astype(f32) + t1[...].astype(f32) + t2[...].astype(f32) + t3[...].astype(f32)
    lane = lanes((TOK, TOK))
    g = total[:, D : D + TOK]
    g = jnp.where(lane < 32, g + pltpu.roll(g, 96, 1), 0.0)
    gate = gates[...]
    picked = gate * (g - jnp.sum(gate * g, axis=-1, keepdims=True))
    low = picked.astype(bf16)
    grad = total[:, 0:D] + nt(low, w[:, 256:384])
    h = hidden[...]
    r = lax.rsqrt(jnp.mean(h * h, axis=-1, keepdims=True) + EPS)
    gain_row = jnp.sum(grad * h * r, axis=0, keepdims=True)
    scaled = grad * gain[1:2, :]
    dot = jnp.mean(h * scaled, axis=-1, keepdims=True)
    out = cot[...].astype(f32) + r * scaled - h * (r * r * r * dot)
    hidden_grad[...] = out
    b = out.astype(bf16)
    ag = nt(b, wo[...]).astype(bf16)
    for j in range(8):
        attn_grad[j] = ag[:, TOK * j : TOK * (j + 1)]
    whole[:, 0:D] = tn(attn_low[...], b).astype(bf16)
    router = tn(payload[:, 0:D], low)
    for j in range(8):
        at = slice(TOK * j, TOK * (j + 1))
        col = jnp.transpose(jnp.broadcast_to(gain_row[:, at], (TOK, TOK)))
        whole[at, D : D + TOK] = jnp.where(lane == 32, col, router[at, :]).astype(bf16)
    for k in range(8):
        for n, to in enumerate((own, other)):
            at = pl.multiple_of(where[8 + k + 8 * n] * 64, 64)
            to[k % 4, k // 4] = whole[pl.ds(at, 64), :]


def to_input(x, gain, hidden_grad, t0, t1, t2, t3, out):
    grad = t0[0].astype(f32) + t1[0].astype(f32) + t2[0].astype(f32) + t3[...].astype(f32)
    h = x[...].astype(f32)
    r = lax.rsqrt(jnp.mean(h * h, axis=-1, keepdims=True) + EPS)
    scaled = grad * gain[0:1, :]
    dot = jnp.mean(h * scaled, axis=-1, keepdims=True)
    out[...] = hidden_grad[...] + r * scaled - h * (r * r * r * dot)


def column_as_row(column):
    return jnp.transpose(jnp.broadcast_to(column, (64, TOK)))[0:1, :]


def finished(rho, wq, wkv, gain, *refs):
    parts = refs[:8]
    out_q, out_kv, out_o, out_router, out_moe, out_gain, pairs = refs[8:]
    total = jnp.zeros((64, D + TOK), f32)
    for k in range(8):
        total = total + parts[k][:, 0 : D + TOK].astype(f32)
        at = rho[k]
        out_q[:, pl.ds(pl.multiple_of(at * TOK, TOK), TOK)] = parts[k][
            :, D + TOK : D + 2 * TOK
        ].astype(f32)
        pairs[at] = parts[k][:, D + 2 * TOK : D + 3 * TOK].astype(f32)
    out_o[...] = total[:, 0:D]
    out_router[...] = jnp.transpose(total[:, D : D + TOK])[0:EXPERTS, :]
    out_moe[...] = column_as_row(total[:, D + EXPERTS : D + EXPERTS + 1])
    first = lanes((64, TOK)) < HD
    for j in range(4):
        a, b = pairs[2 * j], pairs[2 * j + 1]
        out_kv[:, TOK * j : TOK * (j + 1)] = jnp.where(first, a, pltpu.roll(b, HD, 1))
        out_kv[:, 512 + TOK * j : 512 + TOK * (j + 1)] = jnp.where(first, pltpu.roll(a, HD, 1), b)
    both = out_q[...] * wq[...].astype(f32) + out_kv[...] * wkv[...].astype(f32)
    out_gain[...] = column_as_row(jnp.sum(both, axis=-1, keepdims=True)) / gain[...].astype(f32)


def body(
    layer_input,
    cotangent,
    gain_attn,
    w_query,
    w_keyval,
    w_output,
    gain_moe,
    w_router,
    w_in,
    w_out,
    routes,
    priority,
    block_ids,
):
    x = layer_input.reshape(TOK, D)
    cot = cotangent.reshape(TOK, D)
    route_rows = routes.reshape(TOK, TOPK)
    order_row = priority.reshape(1, TOK)
    marks = block_ids.reshape(1, TOK)
    where = lax.dynamic_index_in_dim(
        jnp.asarray(places()), lax.axis_index(tuple(SIZES)), keepdims=False
    )

    payload, small = call(
        prepare,
        "prepare",
        [where],
        [
            x,
            block_ids.reshape(1, TOK),
            w_query,
            w_keyval,
            w_router.T,
            gain_attn.reshape(1, 64),
            gain_moe.reshape(1, 64),
        ],
        [struct((TOK + 16, D), bf16), struct((16, 64, 384), bf16)],
        us=2,
    )
    xs = spread(payload, "xl", "z")
    small = lax.all_to_all(small, SHARD, 0, 0, tiled=True).reshape(D, 384)
    early = lax.all_gather(jnp.concatenate([w_output, cot], axis=0), SHARD, axis=0)
    cos, sin = (jnp.asarray(t) for t in rope_tables())
    norm, q, kv, attn, low_cols, lse, gain, seq_marks = call(
        attend,
        "attend",
        [where],
        [small, cos, sin, *xs],
        [
            struct((LEN, D), bf16),
            struct((LEN, 128), bf16),
            struct((LEN, 128), bf16),
            struct((LEN, 128), f32),
            struct((LEN, 128), bf16),
            struct((LEN, 128), f32),
            struct((8, D), f32),
            struct((8, TOK), f32),
        ],
        us=10,
    )
    attn_in = lax.all_to_all(low_cols.reshape(8, TOK, 128), REP, 0, 0, tiled=True)
    wo, low, hidden, payload, gates = call(
        to_experts,
        "to_experts",
        [],
        [x, attn_in, route_rows, order_row, gain, small, early],
        [
            struct((D, D), bf16),
            struct((TOK, D), bf16),
            struct((TOK, D), f32),
            struct((TOK, D + TOK), bf16),
            struct((TOK, TOK), f32),
        ],
        [pltpu.SemaphoreType.DMA((16,))],
        far=1,
        us=5,
    )
    tokens = spread(payload, "xh", "y")
    tokens = tokens + [cross(t, "c") for t in tokens]
    sums = [struct((4, TOK, D + TOK), bf16)] * 4
    own_0, other_0, own_1, other_1, parts, own_r, other_r = call(
        experts,
        "experts",
        [where],
        [*tokens, w_in, w_out, early],
        [*sums, struct((8, 384, D), bf16), *[struct((4, 2, TOK, D), bf16)] * 2],
        [
            *[pltpu.VMEM(k.shape, k.dtype) for k in sums],
            pltpu.VMEM((2, SLOTS, F), bf16),
            pltpu.VMEM((2, SLOTS, 2 * F), bf16),
            pltpu.VMEM((2, SLOTS, D), bf16),
            pltpu.VMEM((8, 4 * CAP, 256), bf16),
            pltpu.VMEM((2, SLOTS, D), bf16),
            pltpu.VMEM((2, SLOTS, D), bf16),
            pltpu.VMEM((2, D, 2 * F), bf16),
            pltpu.VMEM((2, F, D), bf16),
            pltpu.VMEM((16, TOK, D + TOK), bf16),
            pltpu.VMEM((16, TOK, D), bf16),
            pltpu.VMEM((256, TOK), f32),
            pltpu.VMEM((2, SLOTS, D), bf16),
            pltpu.VMEM((2, SLOTS, 1), f32),
            pltpu.VMEM((2, SLOTS, D), bf16),
            pltpu.VMEM((2, SLOTS, TOK), bf16),
            pltpu.SemaphoreType.DMA((16,)),
            pltpu.SemaphoreType.DMA((16,)),
            pltpu.SemaphoreType.DMA((4,)),
            pltpu.SemaphoreType.DMA((4,)),
            pltpu.SemaphoreType.DMA((16,)),
            pltpu.SemaphoreType.DMA((2, 16)),
        ],
        us=27,
        vmem=60,
        far=19,
        far_outs=7,
    )
    far = added(own_1, cross(other_1, "c"), "far_sums")
    near = added(own_0, cross(other_0, "c"), "near_sums")
    slot_terms = collect_fast(near, far, "xh", "y")
    r_pairs = added(own_r, cross(other_r, "c"), "result_sums", us=4)
    r_terms, r_step = collect(*r_pairs, "xh", "y")
    expert_sum = lax.psum_scatter(parts.reshape(-1, D), REP, scatter_dimension=0, tiled=True)
    attn_grad, hidden_grad, dense_own, dense_other = call(
        from_experts,
        "from_experts",
        [where],
        [*slot_terms, gates, hidden, cot, gain, small, wo, low, payload],
        [
            struct((8, TOK, 128), bf16),
            struct((TOK, D), f32),
            *[struct((4, 2, 64, D + TOK), bf16)] * 2,
        ],
        [pltpu.VMEM((D, D + TOK), bf16)],
        us=6,
        after=[r_pairs[0]],
    )
    attn_grad = lax.all_to_all(attn_grad, REP, 0, 0, tiled=True).reshape(LEN, 128)
    dense = added(dense_own, cross(dense_other, "c"), "dense_sums", us=3)
    dense_terms, dense_step = collect(*dense, "xh", "y")
    first = call(
        attend_back_0,
        "attend_back_0",
        [],
        [q, kv, attn, lse, attn_grad, seq_marks],
        [struct((LEN, 128), f32)] * 3,
        us=60,
    )
    wgrad, *norm_terms = call(
        attend_back_1,
        "attend_back_1",
        [where],
        [cos, sin, q, kv, attn, lse, attn_grad, seq_marks, *first, small, norm],
        [struct((D, 256), bf16), *[struct((2, TOK, D), bf16)] * 4],
        [pltpu.VMEM((LEN, 256), bf16), *[pltpu.VMEM((LEN, 128), f32)] * 3],
        us=10,
        after=[dense_step],
    )
    wgrad = lax.all_to_all(wgrad.reshape(16, 64, 256), SHARD, 0, 0, tiled=True)
    norm_terms, norm_step = collect(*norm_terms, "xl", "z")
    result = call(
        layer_result, "layer_result", [], [hidden, *r_terms], [struct((TOK, D), bf16)]
    )[0]
    grad_in, grad_out = call(
        expert_grads,
        "expert_grads",
        [],
        [expert_sum],
        [struct((2, TOK, D), f32), struct((2, 64, D), f32)],
    )
    last = call(
        last_terms,
        "last_terms",
        [],
        [wgrad, *dense_terms],
        [struct((64, D + 3 * TOK), bf16)],
        after=[norm_step, result, grad_in],
        us=2,
    )[0]
    last = spread(last, "xl", "z")
    grad_input = call(
        to_input,
        "to_input",
        [],
        [x, gain, hidden_grad, *norm_terms],
        [struct((TOK, D), f32)],
    )[0]
    grad_q, grad_kv, grad_o, grad_router, grad_moe, grad_gain = call(
        finished,
        "finished",
        [where],
        [w_query, w_keyval, gain_attn.reshape(1, 64), *last],
        [
            struct((64, D), f32),
            struct((64, D), f32),
            struct((64, D), f32),
            struct((EXPERTS, 64), f32),
            struct((1, 64), f32),
            struct((1, 64), f32),
        ],
        [pltpu.VMEM((8, 64, TOK), f32)],
    )
    return (
        result.reshape(layer_input.shape),
        grad_input.reshape(layer_input.shape),
        grad_gain.reshape(64),
        grad_q,
        grad_kv,
        grad_o,
        grad_moe.reshape(64),
        grad_router.T,
        grad_in,
        grad_out,
    )


def solution(mesh):
    split = Mesh(mesh.devices.reshape(tuple(SIZES.values())), tuple(SIZES))
    tokens = P(SHARD, REP, None)
    weight = P(SHARD, None)
    return jax.shard_map(
        body,
        mesh=split,
        in_specs=(
            tokens,
            tokens,
            P(SHARD),
            weight,
            weight,
            weight,
            P(SHARD),
            weight,
            P(SHARD, None, None),
            P(SHARD, None, None),
            tokens,
            tokens,
            P(SHARD, REP),
        ),
        out_specs=(
            tokens,
            tokens,
            P(SHARD),
            weight,
            weight,
            weight,
            P(SHARD),
            weight,
            tokens,
            tokens,
        ),
        check_vma=False,
    )
```

```python
import itertools

import jax
import jax.numpy as jnp
import numpy as np
from jax import lax
from jax.experimental import pallas as pl
from jax.experimental.pallas import tpu as pltpu
from jax.sharding import Mesh
from jax.sharding import PartitionSpec as P

HEADS = 16
KV = 8
HD = 64
EXPERTS = 32
TOPK = 8
CAP = 40
TOK = 128
D = 1024
F = 512
LEN = 1024
EPS = 1e-06
SHARD = ("xh", "y", "c")
REP = ("xl", "z")
SIZES = {"xh": 2, "y": 4, "c": 2, "xl": 2, "z": 4}
bf16 = jnp.bfloat16
f32 = jnp.float32

VM = pl.BlockSpec(memory_space=pltpu.VMEM)
SM = pl.BlockSpec(memory_space=pltpu.SMEM)
ANY = pl.BlockSpec(memory_space=pl.ANY)


def moved(x, axes, to):
    sizes = [SIZES[a] for a in axes]
    pairs = []
    for here in itertools.product(*[range(s) for s in sizes]):
        there = to(*here)
        a = b = 0
        for s, i, j in zip(sizes, here, there):
            a, b = a * s + i, b * s + j % s
        pairs.append((a, b))
    return lax.ppermute(x, axes, pairs)


def ring(x, axis, sign):
    if axis == "y":
        return moved(x, ("y", "c"), lambda y, c: (y + sign * (1 - 2 * c), c))
    return moved(x, ("c", "z"), lambda c, z: (c, z + sign * (1 - 2 * c)))


def cross(x, axis):
    return moved(x, (axis,), lambda i: (1 - i,))


def spread(x, pair, axis):
    across = cross(x, pair)
    a = ring(x, axis, 1)
    b = ring(x, axis, -1)
    xa = ring(across, axis, 1)
    xb = ring(across, axis, -1)
    a2 = ring(a, axis, 1)
    xa2 = ring(xa, axis, 1)
    return [x, a, b, a2, across, xa, xb, xa2]


def owners(pair, ring_at, core):
    way = 1 - 2 * core
    return [p * 4 + (ring_at + s * way) % 4 for p in (pair, 1 - pair) for s in (0, -1, 1, -2)]


def places():
    table = []
    for xh, y, c, xl, z in itertools.product(*[range(s) for s in SIZES.values()]):
        mine = [2 * o + c for o in owners(xh, y, c)]
        other = [2 * o + 1 - c for o in owners(xh, y, 1 - c)]
        table.append([*owners(xl, z, c), *mine, *other, (xh * 4 + y) * 2 + c, xl * 4 + z, *[0] * 6])
    return np.array(table, np.int32)


def plus(*terms):
    total = terms[0].astype(f32)
    for t in terms[1:]:
        total = total + t.astype(f32)
    return total.astype(bf16)


def plus_after(a, b, after):
    def kernel(a, b, out):
        out[...] = (a[...].astype(f32) + b[...].astype(f32)).astype(bf16)

    return call(kernel, "plus_after", [], [a, b], [struct(a.shape, bf16)], us=1, after=[after])[0]


def collect(own, a, b, a2, pair, axis, after=None):
    from_b = ring(b, axis, 1)
    arrived = ring(a2, axis, -1)
    step = plus(a, arrived) if after is None else plus_after(a, arrived, after)
    from_a = ring(step, axis, -1)
    return [own, from_b, from_a, cross(plus(own[1], from_b[1], from_a[1]), pair)], step


def collect_fast(near, far, pair, axis):
    r2 = ring(far[3], axis, -1)
    rb = ring(far[2], axis, 1)
    s2 = ring(near[3], axis, -1)
    sb = ring(near[2], axis, 1)
    ra = ring(plus(far[1], r2), axis, -1)
    sa = ring(plus(near[1], s2), axis, -1)
    return [near[0], sb, sa, cross(plus(far[0], rb, ra), pair)]


def nn(a, b):
    return jnp.dot(a, b, preferred_element_type=f32)


def nt(a, b):
    return lax.dot_general(a, b, (((1,), (1,)), ((), ())), preferred_element_type=f32)


def tn(a, b):
    return lax.dot_general(a, b, (((0,), (0,)), ((), ())), preferred_element_type=f32)


def lanes(shape):
    return lax.broadcasted_iota(jnp.int32, shape, len(shape) - 1)


def rows(shape):
    return lax.broadcasted_iota(jnp.int32, shape, 0)


def call(
    kernel, name, scalars, arrays, outs, scratch=(), us=3, vmem=56, far=0, far_outs=0, after=()
):
    given = len(scalars) + len(arrays)

    def run(*refs):
        kernel(*refs[:given], *refs[given + len(after) :])

    return pl.pallas_call(
        run,
        name=name,
        out_shape=outs,
        in_specs=[SM] * len(scalars) + [VM] * (len(arrays) - far) + [ANY] * (far + len(after)),
        out_specs=[ANY] * far_outs + [VM] * (len(outs) - far_outs),
        scratch_shapes=list(scratch),
        compiler_params=pltpu.CompilerParams(vmem_limit_bytes=vmem << 20),
        cost_estimate=pl.CostEstimate(
            flops=0, bytes_accessed=us * 3690000, transcendentals=0
        ),
    )(*scalars, *arrays, *after)


def struct(shape, dtype):
    return jax.ShapeDtypeStruct(shape, dtype)


def rope_tables():
    half = HD // 2
    frequency = np.power(10000.0, np.arange(half) * (-2.0 / HD))
    angles = np.arange(LEN)[:, None] * frequency[None, :]
    cosine, sine = np.cos(angles), np.sin(angles)
    return (
        np.concatenate([cosine] * 4, axis=1).astype(np.float32),
        np.concatenate([-sine, sine, -sine, sine], axis=1).astype(np.float32),
    )


def halves_swapped(x):
    first = lanes(x.shape) % HD < HD // 2
    return jnp.where(first, pltpu.roll(x, 96, 1), pltpu.roll(x, 32, 1))


def block_column(marks, j):
    return jnp.transpose(jnp.broadcast_to(marks[j : j + 1, :], (TOK, TOK)))[:, 0:1]


QB = 256


def visible_of(marks, i):
    reach = min(LEN, QB * (i + 2))
    row = jnp.concatenate([marks[j : j + 1, :] for j in range(reach // TOK)], axis=1)
    col = jnp.concatenate(
        [block_column(marks, j) for j in range(QB // TOK * i, QB // TOK * (i + 1))], axis=0
    )
    return reach, row <= col


def prepare(where, x, marks, wq, wkv, router, gain_a, gain_m, payload, small):
    payload[0:TOK, :] = x[...]
    payload[TOK : TOK + 16, :] = jnp.zeros((16, D), bf16)
    ids = jnp.where(rows((16, TOK)) == 0, marks[...].astype(f32), 0.0)
    payload[TOK : TOK + 16, 0:TOK] = ids.astype(bf16)
    rep = where[25]
    mine = pl.ds(pl.multiple_of(rep * 128, 128), 128)
    pair = lax.div(rep, 2)
    odd = jnp.full((64, 128), lax.rem(rep, 2)) == 1
    key = wkv[:, pl.ds(pl.multiple_of(pair * 128, 128), 128)].astype(f32)
    value = wkv[:, pl.ds(pl.multiple_of(512 + pair * 128, 128), 128)].astype(f32)
    key = jnp.where(odd, pltpu.roll(key, HD, 1), key)
    value = jnp.where(odd, value, pltpu.roll(value, HD, 1))
    kv = jnp.where(lanes((64, 128)) < HD, key, value).astype(bf16)
    diagonal = rows((64, 64)) == lanes((64, 64))
    gains = []
    for gain in (gain_a, gain_m):
        row = jnp.broadcast_to(gain[...].astype(f32), (64, 64))
        gains.append(jnp.sum(jnp.where(diagonal, row, 0.0), axis=1, keepdims=True))
    lane = lanes((64, 128))
    one = (rows((EXPERTS, 128)) == lanes((EXPERTS, 128))).astype(f32).astype(bf16)
    extra = tn(router[...], one)
    extra = jnp.where(lane == 32, gains[0], jnp.where(lane == 33, gains[1], extra)).astype(bf16)
    q = wq[:, mine]
    for n in range(16):
        small[n, :, 0:128] = q
        small[n, :, 128:256] = kv
        small[n, :, 256:384] = extra


def attend(rho, w, cos, sin, *refs):
    xs = refs[:8]
    norm, q_out, kv_out, attn_out, low_out, lse_out, gain_out, marks_out = refs[8:16]
    for j in range(8):
        part = jnp.transpose(w[TOK * j : TOK * (j + 1), 256:384].astype(f32))
        gain_out[0:8, TOK * j : TOK * (j + 1)] = part[32:40, :]
    gain = gain_out[0:1, :]
    for k in range(8):
        at = rho[k]
        marks_out[pl.ds(at, 1), :] = xs[k][TOK : TOK + 16, 0:TOK].astype(f32)[0:1]
        x = xs[k][0:TOK, :].astype(f32)
        inv = lax.rsqrt(jnp.mean(x * x, axis=-1, keepdims=True) + EPS)
        norm[pl.ds(pl.multiple_of(at * TOK, TOK), TOK), :] = (x * inv * gain).astype(bf16)
    marks = marks_out[...]
    pre = nn(norm[...], w[:, 0:256])
    c, s = cos[...], sin[...]
    q = pre[:, 0:128]
    q_out[...] = ((q * c + halves_swapped(q) * s) * (HD**-0.5)).astype(bf16)
    kv = pre[:, 128:256]
    is_key = lanes(kv.shape) < HD
    kv_out[...] = jnp.where(is_key, kv * c + halves_swapped(kv) * s, kv).astype(bf16)
    kvf = kv_out[...].astype(f32)
    turned = pltpu.roll(kvf, HD, 1)
    keys = jnp.where(is_key, kvf, turned).astype(bf16)
    values = jnp.where(is_key, turned, kvf).astype(bf16)
    for i in range(LEN // QB):
        reach, visible = visible_of(marks, i)
        at = slice(QB * i, QB * (i + 1))
        qi = q_out[at, :]
        first = lanes(qi.shape) < HD
        mixed, logs = [], []
        for h in range(2):
            qh = jnp.where(first == (h == 0), qi, jnp.zeros_like(qi))
            scores = jnp.where(visible, nt(qh, keys[:reach]), -1e30)
            top = jnp.max(scores, axis=-1, keepdims=True)
            e = jnp.exp(scores - top)
            total = jnp.sum(e, axis=-1, keepdims=True)
            mixed.append(nn(e.astype(bf16), values[:reach]) / total)
            logs.append(top + jnp.log(total))
        attn = jnp.where(first, mixed[0], mixed[1])
        attn_out[at, :] = attn
        low_out[at, :] = attn.astype(bf16)
        lse_out[at, :] = jnp.where(first, logs[0], logs[1])


def head_back(h, q, kv, attn, lse, grad, marks, dq, dk, dv):
    kvf = kv[...].astype(f32)
    is_key = lanes(kvf.shape) < HD
    turned = pltpu.roll(kvf, HD, 1)
    keys = jnp.where(is_key, kvf, turned).astype(bf16)
    values = jnp.where(is_key, turned, kvf).astype(bf16)
    for i in range(LEN // QB):
        reach, visible = visible_of(marks, i)
        at = slice(QB * i, QB * (i + 1))
        qi, gi = q[at, :], grad[at, :]
        mine = (lanes(qi.shape) < HD) == (h == 0)
        qh = jnp.where(mine, qi, jnp.zeros_like(qi))
        gh = jnp.where(mine, gi, jnp.zeros_like(gi))
        part = jnp.where(mine, gi.astype(f32) * attn[at, :], 0.0)
        delta = jnp.sum(part, axis=-1, keepdims=True)
        scores = nt(qh, keys[:reach])
        log = lse[at, HD * h : HD * h + 1]
        weights = jnp.where(visible, jnp.exp(scores - log), 0.0)
        low = (weights * (nt(gh, values[:reach]) - delta)).astype(bf16)
        dq[at, :] = jnp.where(mine, nn(low, keys[:reach]), dq[at, :])
        dk[:reach, :] += tn(low, qh)
        dv[:reach, :] += tn(weights.astype(bf16), gh)


def attend_back_0(q, kv, attn, lse, grad, marks_in, dq, dk, dv):
    dq[...] = jnp.zeros_like(dq)
    dk[...] = jnp.zeros_like(dk)
    dv[...] = jnp.zeros_like(dv)
    head_back(0, q, kv, attn, lse, grad, marks_in[...], dq, dk, dv)


def attend_back_1(where, cos, sin, q, kv, attn, lse, grad, marks_in, dq_in, dk_in, dv_in, w, norm, *refs):
    (wgrad, *pairs), (out, dq, dk, dv) = refs[:5], refs[5:]
    dq[...] = dq_in[...]
    dk[...] = dk_in[...]
    dv[...] = dv_in[...]
    head_back(1, q, kv, attn, lse, grad, marks_in[...], dq, dk, dv)
    c, s = cos[...], sin[...]
    g = dq[...] * (HD**-0.5)
    out[:, 0:128] = (g * c - halves_swapped(g) * s).astype(bf16)
    key = dk[...]
    key = key + pltpu.roll(key, HD, 1)
    val = dv[...]
    val = val + pltpu.roll(val, HD, 1)
    key = key * c - halves_swapped(key) * s
    out[:, 128:256] = jnp.where(lanes(key.shape) < HD, key, val).astype(bf16)
    wgrad[...] = tn(norm[...], out[...]).astype(bf16)
    for k in range(8):
        at = pl.multiple_of(where[k] * TOK, TOK)
        pairs[k % 4][k // 4] = nt(out[pl.ds(at, TOK), :], w[:, 0:256]).astype(bf16)


def to_experts(
    x, attn, routes, priority, gain, w, early, wo, low, hidden, payload, gates_out, sems
):
    copies = []
    for s in range(16):
        to = wo.at[64 * s : 64 * (s + 1), :]
        copies.append(pltpu.make_async_copy(early.at[s, 0:64, :], to, sems.at[s]))
        copies[-1].start()
    for r in range(8):
        low[:, TOK * r : TOK * (r + 1)] = attn[r]
    for copy in copies:
        copy.wait()
    h = x[...].astype(f32) + nn(low[...], wo[...])
    hidden[...] = h
    inv = lax.rsqrt(jnp.mean(h * h, axis=-1, keepdims=True) + EPS)
    normed = (h * inv * gain[1:2, :]).astype(bf16)
    payload[:, 0:D] = normed
    logits = nn(normed, w[:, 256:384])
    lane = lanes((TOK, TOK))
    member = lane == routes[:, 0:1]
    for k in range(1, TOPK):
        member = member | (lane == routes[:, k : k + 1])
    order = jnp.broadcast_to(priority[...], (TOK, TOK)).astype(f32)
    earlier = (order < jnp.transpose(order)).astype(f32).astype(bf16)
    before = nn(earlier, member.astype(f32).astype(bf16))
    kept = member & (before < CAP)
    top = jnp.max(jnp.where(member, logits, -1e30), axis=-1, keepdims=True)
    e = jnp.where(member, jnp.exp(jnp.where(member, logits - top, 0.0)), 0.0)
    gates = e / jnp.sum(e, axis=-1, keepdims=True)
    gates_out[...] = gates
    high = gates.astype(bf16).astype(f32)
    rank = jnp.where(kept, before, -1.0)
    meta = jnp.where(
        lane < 32,
        rank,
        jnp.where(lane < 64, pltpu.roll(high, 32, 1), pltpu.roll(gates - high, 64, 1)),
    )
    payload[:, D : D + TOK] = jnp.transpose(meta).astype(bf16)


SLOTS = 16 * CAP


def assignment(pair, xb, meta, first, gate_col, at):
    two = 2 * CAP
    side = rows((two, 256)) >= CAP
    place = (rows((two, 256)) - jnp.where(side, CAP, 0)).astype(f32)
    here = side == (lanes((two, 256)) >= TOK)
    chosen = []
    for n, k in enumerate(pair):
        meta[TOK * n : TOK * (n + 1), :] = xb[k, :, D : D + TOK].astype(f32)
    for e in range(2):
        def line(offset):
            return jnp.concatenate(
                [meta[pl.ds(TOK * n + offset + first + e, 1), :] for n in range(2)], axis=1
            )

        pick = jnp.where((line(0) == place) & here, 1.0, 0.0)
        gate_col[e, at, :] = jnp.sum(pick * (line(32) + line(64)), axis=-1, keepdims=True)
        chosen.append(pick.astype(bf16))
    return jnp.concatenate(chosen, axis=0)


def fetches(who, xs, xb, x_sem, early, cb, c_sem):
    x_in = [pltpu.make_async_copy(xs[k], xb.at[k], x_sem.at[k]) for k in range(16)]
    c_in = []
    for k in range(16):
        source = early.at[who[8 + k], 64:192, :]
        c_in.append(pltpu.make_async_copy(source, cb.at[k], c_sem.at[k]))
    return x_in, c_in


def experts(who, *refs):
    xs, (w_in_far, w_out_far, cot_far) = refs[:16], refs[16:19]
    sums_far, (parts, own_r, other_r), sums = refs[19:23], refs[23:26], refs[26:30]
    act_o, pre_g, outs, picks, disp, out_g = refs[30:36]
    w_in, w_out, xb, cb, meta, cot_rows, gate_col, back, gg = refs[36:45]
    x_sem, c_sem, w_sem, o_sem, r_sem, g_sem = refs[45:]
    first = who[24] * 2
    two = 2 * CAP
    x_in, c_in = fetches(who, xs, xb, x_sem, cot_far, cb, c_sem)
    w_copies = []
    for e in range(2):
        w_copies.append(pltpu.make_async_copy(w_in_far.at[e], w_in.at[e], w_sem.at[2 * e]))
        w_copies.append(pltpu.make_async_copy(w_out_far.at[e], w_out.at[e], w_sem.at[2 * e + 1]))
    for p in range(8):
        x_in[p].start()
        x_in[p + 8].start()
    w_copies[0].start()
    w_copies[1].start()
    for p in range(8):
        c_in[p].start()
        c_in[p + 8].start()
    w_copies[2].start()
    w_copies[3].start()
    leaving = []

    def leave(source, to, sem):
        leaving.append(pltpu.make_async_copy(source, to, sem))
        leaving[-1].start()

    for p in range(8):
        at = slice(two * p, two * (p + 1))
        pair = (p, p + 8)
        for k in pair:
            x_in[k].wait()
        pick = assignment(pair, xb, meta, first, gate_col, at)
        picks[p] = pick
        found = nn(pick, jnp.concatenate([xb[k, :, 0:D] for k in pair], axis=0)).astype(bf16)
        for e in range(2):
            disp[e, at, :] = found[two * e : two * (e + 1)]
    for e in range(2):
        w_copies[2 * e].wait()
        pre = nn(disp[e], w_in[e])
        gate, up = pre[:, 0:F], pre[:, F : 2 * F]
        sig = 1.0 / (1.0 + jnp.exp(-gate))
        silu = gate * sig
        act = (silu * up).astype(bf16)
        act_o[e] = act
        w_copies[2 * e + 1].wait()
        out = nn(act, w_out[e])
        if e == 0:
            for p in range(8):
                at = slice(two * p, two * (p + 1))
                c_in[p].wait()
                c_in[p + 8].wait()
                cot = nn(picks[p], jnp.concatenate([cb[p], cb[p + 8]], axis=0))
                for n in range(2):
                    part = cot[two * n : two * (n + 1)]
                    cot_rows[n, at, :] = part.astype(bf16)
                    out_g[n, at, :] = (gate_col[n, at, :] * part).astype(bf16)
        g = jnp.sum(out * cot_rows[e].astype(f32), axis=-1, keepdims=True)
        high = g.astype(bf16).astype(f32)
        lane = lanes((SLOTS, TOK))
        gg[e] = jnp.where(
            lane == first + e, high, jnp.where(lane == first + e + 32, g - high, 0.0)
        ).astype(bf16)
        outs[e] = (gate_col[e] * out).astype(bf16)
        act_grad = nt(out_g[e], w_out[e])
        d_up = act_grad * silu
        d_gate = act_grad * up * (sig * (1.0 + gate * (1.0 - sig)))
        pre_g[e, :, 0:F] = d_gate.astype(bf16)
        pre_g[e, :, F : 2 * F] = d_up.astype(bf16)
        back[e] = nt(pre_g[e], w_in[e]).astype(bf16)
    for half in (1, 0):
        for p in range(4 * half, 4 * half + 4):
            at = slice(two * p, two * (p + 1))
            slot = jnp.concatenate([back[0, at, :], back[1, at, :]], axis=0)
            grads = jnp.concatenate([gg[0, at, :], gg[1, at, :]], axis=0)
            for n in range(2):
                whole = sums[2 * half + n].at[p % 4]
                pick = picks[p, :, TOK * n : TOK * (n + 1)]
                whole[:, 0:D] = tn(pick, slot).astype(bf16)
                whole[:, D : D + TOK] = tn(pick, grads).astype(bf16)
        for n in (2 * half + 1, 2 * half):
            leave(sums[n], sums_far[n], o_sem.at[n])
    for p in range(8):
        at = slice(two * p, two * (p + 1))
        value = jnp.concatenate([outs[0, at, :], outs[1, at, :]], axis=0)
        for n, to in enumerate((own_r, other_r)):
            k = p + 8 * n
            cb[k] = tn(picks[p, :, TOK * n : TOK * (n + 1)], value).astype(bf16)
            leave(cb.at[k], to.at[p % 4, p // 4], r_sem.at[k])

    far = who[25] // 4

    def send(grad, e, count, row):
        for k in range(8):
            to = parts.at[2 * (k % 4) + lax.bitwise_xor(k // 4, far), row : row + count, :]
            sem = g_sem.at[e, k + 8 * (count == 64)]
            leave(grad.at[e, count * k : count * (k + 1), :], to, sem)

    for e in range(2):
        w_in[e] = tn(disp[e], pre_g[e]).astype(bf16)
        send(w_in, e, TOK, TOK * e)
        w_out[e] = tn(act_o[e], out_g[e]).astype(bf16)
        send(w_out, e, 64, 256 + 64 * e)
    for copy in leaving:
        copy.wait()


def second_half(whole, after):
    def kernel(a, _, out):
        out[...] = a[...]

    return pl.pallas_call(
        kernel,
        name="second_half",
        out_shape=struct((384, D), bf16),
        grid=(1,),
        in_specs=[pl.BlockSpec((384, D), lambda i: (1, 0)), ANY],
        out_specs=pl.BlockSpec((384, D), lambda i: (0, 0)),
    )(whole, after)


def expert_grads(a, b, grad_in, grad_out):
    for e in range(2):
        at = slice(TOK * e, TOK * (e + 1))
        grad_in[e] = a[at, :].astype(f32) + b[at, :].astype(f32)
        at = slice(256 + 64 * e, 320 + 64 * e)
        grad_out[e] = a[at, :].astype(f32) + b[at, :].astype(f32)


def added(a, b, name, us=2):
    count = a.shape[0]

    def kernel(a_ref, b_ref, *outs):
        for n, out in enumerate(outs):

            @pl.when(pl.program_id(0) == n)
            def _(out=out):
                out[...] = (a_ref[0].astype(f32) + b_ref[0].astype(f32)).astype(bf16)

    zeros = (0,) * (a.ndim - 1)
    block = pl.BlockSpec((1, *a.shape[1:]), lambda i: (i, *zeros))
    return pl.pallas_call(
        kernel,
        name=name,
        out_shape=[struct(a.shape[1:], bf16)] * count,
        grid=(count,),
        in_specs=[block, block],
        out_specs=[pl.BlockSpec(a.shape[1:], lambda i: zeros)] * count,
        compiler_params=pltpu.CompilerParams(vmem_limit_bytes=32 << 20),
        cost_estimate=pl.CostEstimate(
            flops=0, bytes_accessed=us * 3690000, transcendentals=0
        ),
    )(a, b)


def layer_result(hidden, t0, t1, t2, t3, result):
    total = t0[0].astype(f32) + t1[0].astype(f32) + t2[0].astype(f32) + t3[...].astype(f32)
    result[...] = (hidden[...] + total).astype(bf16)


def last_terms(wgrad, t0, t1, t2, t3, last):
    total = t0[0].astype(f32) + t1[0].astype(f32) + t2[0].astype(f32) + t3[...].astype(f32)
    last[:, 0 : D + TOK] = total.astype(bf16)
    last[:, D + TOK :] = sum(wgrad[n].astype(f32) for n in range(16)).astype(bf16)


def from_experts(where, t0, t1, t2, t3, gates, hidden, cot, gain, w, wo, attn_low, payload, *refs):
    attn_grad, hidden_grad, own, other, whole = refs
    total = t0[...].astype(f32) + t1[...].astype(f32) + t2[...].astype(f32) + t3[...].astype(f32)
    lane = lanes((TOK, TOK))
    g = total[:, D : D + TOK]
    g = jnp.where(lane < 32, g + pltpu.roll(g, 96, 1), 0.0)
    gate = gates[...]
    picked = gate * (g - jnp.sum(gate * g, axis=-1, keepdims=True))
    low = picked.astype(bf16)
    grad = total[:, 0:D] + nt(low, w[:, 256:384])
    h = hidden[...]
    r = lax.rsqrt(jnp.mean(h * h, axis=-1, keepdims=True) + EPS)
    gain_row = jnp.sum(grad * h * r, axis=0, keepdims=True)
    scaled = grad * gain[1:2, :]
    dot = jnp.mean(h * scaled, axis=-1, keepdims=True)
    out = cot[...].astype(f32) + r * scaled - h * (r * r * r * dot)
    hidden_grad[...] = out
    b = out.astype(bf16)
    ag = nt(b, wo[...]).astype(bf16)
    for j in range(8):
        attn_grad[j] = ag[:, TOK * j : TOK * (j + 1)]
    whole[:, 0:D] = tn(attn_low[...], b).astype(bf16)
    router = tn(payload[:, 0:D], low)
    for j in range(8):
        at = slice(TOK * j, TOK * (j + 1))
        col = jnp.transpose(jnp.broadcast_to(gain_row[:, at], (TOK, TOK)))
        whole[at, D : D + TOK] = jnp.where(lane == 32, col, router[at, :]).astype(bf16)
    for k in range(8):
        for n, to in enumerate((own, other)):
            at = pl.multiple_of(where[8 + k + 8 * n] * 64, 64)
            to[k % 4, k // 4] = whole[pl.ds(at, 64), :]


def to_input(x, gain, hidden_grad, t0, t1, t2, t3, out):
    grad = t0[0].astype(f32) + t1[0].astype(f32) + t2[0].astype(f32) + t3[...].astype(f32)
    h = x[...].astype(f32)
    r = lax.rsqrt(jnp.mean(h * h, axis=-1, keepdims=True) + EPS)
    scaled = grad * gain[0:1, :]
    dot = jnp.mean(h * scaled, axis=-1, keepdims=True)
    out[...] = hidden_grad[...] + r * scaled - h * (r * r * r * dot)


def column_as_row(column):
    return jnp.transpose(jnp.broadcast_to(column, (64, TOK)))[0:1, :]


def finished(rho, wq, wkv, gain, *refs):
    parts = refs[:8]
    out_q, out_kv, out_o, out_router, out_moe, out_gain, pairs = refs[8:]
    total = jnp.zeros((64, D + TOK), f32)
    for k in range(8):
        total = total + parts[k][:, 0 : D + TOK].astype(f32)
        at = rho[k]
        out_q[:, pl.ds(pl.multiple_of(at * TOK, TOK), TOK)] = parts[k][
            :, D + TOK : D + 2 * TOK
        ].astype(f32)
        pairs[at] = parts[k][:, D + 2 * TOK : D + 3 * TOK].astype(f32)
    out_o[...] = total[:, 0:D]
    out_router[...] = jnp.transpose(total[:, D : D + TOK])[0:EXPERTS, :]
    out_moe[...] = column_as_row(total[:, D + EXPERTS : D + EXPERTS + 1])
    first = lanes((64, TOK)) < HD
    for j in range(4):
        a, b = pairs[2 * j], pairs[2 * j + 1]
        out_kv[:, TOK * j : TOK * (j + 1)] = jnp.where(first, a, pltpu.roll(b, HD, 1))
        out_kv[:, 512 + TOK * j : 512 + TOK * (j + 1)] = jnp.where(first, pltpu.roll(a, HD, 1), b)
    both = out_q[...] * wq[...].astype(f32) + out_kv[...] * wkv[...].astype(f32)
    out_gain[...] = column_as_row(jnp.sum(both, axis=-1, keepdims=True)) / gain[...].astype(f32)


def body(
    layer_input,
    cotangent,
    gain_attn,
    w_query,
    w_keyval,
    w_output,
    gain_moe,
    w_router,
    w_in,
    w_out,
    routes,
    priority,
    block_ids,
):
    x = layer_input.reshape(TOK, D)
    cot = cotangent.reshape(TOK, D)
    route_rows = routes.reshape(TOK, TOPK)
    order_row = priority.reshape(1, TOK)
    marks = block_ids.reshape(1, TOK)
    where = lax.dynamic_index_in_dim(
        jnp.asarray(places()), lax.axis_index(tuple(SIZES)), keepdims=False
    )

    payload, small = call(
        prepare,
        "prepare",
        [where],
        [
            x,
            block_ids.reshape(1, TOK),
            w_query,
            w_keyval,
            w_router.T,
            gain_attn.reshape(1, 64),
            gain_moe.reshape(1, 64),
        ],
        [struct((TOK + 16, D), bf16), struct((16, 64, 384), bf16)],
        us=2,
    )
    xs = spread(payload, "xl", "z")
    small = lax.all_to_all(small, SHARD, 0, 0, tiled=True).reshape(D, 384)
    early = lax.all_gather(jnp.concatenate([w_output, cot], axis=0), SHARD, axis=0)
    cos, sin = (jnp.asarray(t) for t in rope_tables())
    norm, q, kv, attn, low_cols, lse, gain, seq_marks = call(
        attend,
        "attend",
        [where],
        [small, cos, sin, *xs],
        [
            struct((LEN, D), bf16),
            struct((LEN, 128), bf16),
            struct((LEN, 128), bf16),
            struct((LEN, 128), f32),
            struct((LEN, 128), bf16),
            struct((LEN, 128), f32),
            struct((8, D), f32),
            struct((8, TOK), f32),
        ],
        us=10,
    )
    attn_in = lax.all_to_all(low_cols.reshape(8, TOK, 128), REP, 0, 0, tiled=True)
    wo, low, hidden, payload, gates = call(
        to_experts,
        "to_experts",
        [],
        [x, attn_in, route_rows, order_row, gain, small, early],
        [
            struct((D, D), bf16),
            struct((TOK, D), bf16),
            struct((TOK, D), f32),
            struct((TOK, D + TOK), bf16),
            struct((TOK, TOK), f32),
        ],
        [pltpu.SemaphoreType.DMA((16,))],
        far=1,
        us=5,
    )
    tokens = spread(payload, "xh", "y")
    tokens = tokens + [cross(t, "c") for t in tokens]
    sums = [struct((4, TOK, D + TOK), bf16)] * 4
    own_0, other_0, own_1, other_1, parts, own_r, other_r = call(
        experts,
        "experts",
        [where],
        [*tokens, w_in, w_out, early],
        [*sums, struct((8, 384, D), bf16), *[struct((4, 2, TOK, D), bf16)] * 2],
        [
            *[pltpu.VMEM(k.shape, k.dtype) for k in sums],
            pltpu.VMEM((2, SLOTS, F), bf16),
            pltpu.VMEM((2, SLOTS, 2 * F), bf16),
            pltpu.VMEM((2, SLOTS, D), bf16),
            pltpu.VMEM((8, 4 * CAP, 256), bf16),
            pltpu.VMEM((2, SLOTS, D), bf16),
            pltpu.VMEM((2, SLOTS, D), bf16),
            pltpu.VMEM((2, D, 2 * F), bf16),
            pltpu.VMEM((2, F, D), bf16),
            pltpu.VMEM((16, TOK, D + TOK), bf16),
            pltpu.VMEM((16, TOK, D), bf16),
            pltpu.VMEM((256, TOK), f32),
            pltpu.VMEM((2, SLOTS, D), bf16),
            pltpu.VMEM((2, SLOTS, 1), f32),
            pltpu.VMEM((2, SLOTS, D), bf16),
            pltpu.VMEM((2, SLOTS, TOK), bf16),
            pltpu.SemaphoreType.DMA((16,)),
            pltpu.SemaphoreType.DMA((16,)),
            pltpu.SemaphoreType.DMA((4,)),
            pltpu.SemaphoreType.DMA((4,)),
            pltpu.SemaphoreType.DMA((16,)),
            pltpu.SemaphoreType.DMA((2, 16)),
        ],
        us=27,
        vmem=60,
        far=19,
        far_outs=7,
    )
    far = added(own_1, cross(other_1, "c"), "far_sums")
    near = added(own_0, cross(other_0, "c"), "near_sums")
    slot_terms = collect_fast(near, far, "xh", "y")
    r_pairs = added(own_r, cross(other_r, "c"), "result_sums", us=4)
    r_terms, r_step = collect(*r_pairs, "xh", "y")
    expert_sum = lax.psum_scatter(parts.reshape(-1, D), "z", scatter_dimension=0, tiled=True)
    attn_grad, hidden_grad, dense_own, dense_other = call(
        from_experts,
        "from_experts",
        [where],
        [*slot_terms, gates, hidden, cot, gain, small, wo, low, payload],
        [
            struct((8, TOK, 128), bf16),
            struct((TOK, D), f32),
            *[struct((4, 2, 64, D + TOK), bf16)] * 2,
        ],
        [pltpu.VMEM((D, D + TOK), bf16)],
        us=6,
        after=[r_pairs[0]],
    )
    attn_grad = lax.all_to_all(attn_grad, REP, 0, 0, tiled=True).reshape(LEN, 128)
    dense = added(dense_own, cross(dense_other, "c"), "dense_sums", us=3)
    dense_terms, dense_step = collect(*dense, "xh", "y")
    first = call(
        attend_back_0,
        "attend_back_0",
        [],
        [q, kv, attn, lse, attn_grad, seq_marks],
        [struct((LEN, 128), f32)] * 3,
        us=60,
    )
    expert_in = cross(second_half(expert_sum, first[0]), "xl")
    wgrad, *norm_terms = call(
        attend_back_1,
        "attend_back_1",
        [where],
        [cos, sin, q, kv, attn, lse, attn_grad, seq_marks, *first, small, norm],
        [struct((D, 256), bf16), *[struct((2, TOK, D), bf16)] * 4],
        [pltpu.VMEM((LEN, 256), bf16), *[pltpu.VMEM((LEN, 128), f32)] * 3],
        us=10,
        after=[dense_step],
    )
    wgrad = lax.all_to_all(wgrad.reshape(16, 64, 256), SHARD, 0, 0, tiled=True)
    norm_terms, norm_step = collect(*norm_terms, "xl", "z", expert_in)
    result = call(
        layer_result, "layer_result", [], [hidden, *r_terms], [struct((TOK, D), bf16)]
    )[0]
    grad_in, grad_out = call(
        expert_grads,
        "expert_grads",
        [],
        [expert_in, expert_sum],
        [struct((2, TOK, D), f32), struct((2, 64, D), f32)],
    )
    last = call(
        last_terms,
        "last_terms",
        [],
        [wgrad, *dense_terms],
        [struct((64, D + 3 * TOK), bf16)],
        after=[norm_step, result, grad_in],
        us=2,
    )[0]
    last = spread(last, "xl", "z")
    grad_input = call(
        to_input,
        "to_input",
        [],
        [x, gain, hidden_grad, *norm_terms],
        [struct((TOK, D), f32)],
    )[0]
    grad_q, grad_kv, grad_o, grad_router, grad_moe, grad_gain = call(
        finished,
        "finished",
        [where],
        [w_query, w_keyval, gain_attn.reshape(1, 64), *last],
        [
            struct((64, D), f32),
            struct((64, D), f32),
            struct((64, D), f32),
            struct((EXPERTS, 64), f32),
            struct((1, 64), f32),
            struct((1, 64), f32),
        ],
        [pltpu.VMEM((8, 64, TOK), f32)],
        after=[grad_input],
    )
    return (
        result.reshape(layer_input.shape),
        grad_input.reshape(layer_input.shape),
        grad_gain.reshape(64),
        grad_q,
        grad_kv,
        grad_o,
        grad_moe.reshape(64),
        grad_router.T,
        grad_in,
        grad_out,
    )


def solution(mesh):
    split = Mesh(mesh.devices.reshape(tuple(SIZES.values())), tuple(SIZES))
    tokens = P(SHARD, REP, None)
    weight = P(SHARD, None)
    return jax.shard_map(
        body,
        mesh=split,
        in_specs=(
            tokens,
            tokens,
            P(SHARD),
            weight,
            weight,
            weight,
            P(SHARD),
            weight,
            P(SHARD, None, None),
            P(SHARD, None, None),
            tokens,
            tokens,
            P(SHARD, REP),
        ),
        out_specs=(
            tokens,
            tokens,
            P(SHARD),
            weight,
            weight,
            weight,
            P(SHARD),
            weight,
            tokens,
            tokens,
        ),
        check_vma=False,
    )
```

```python
import itertools

import jax
import jax.numpy as jnp
import numpy as np
from jax import lax
from jax.experimental import pallas as pl
from jax.experimental.pallas import tpu as pltpu
from jax.sharding import Mesh
from jax.sharding import PartitionSpec as P

HEADS = 16
KV = 8
HD = 64
EXPERTS = 32
TOPK = 8
CAP = 40
TOK = 128
D = 1024
F = 512
LEN = 1024
EPS = 1e-06
SHARD = ("xh", "y", "c")
REP = ("xl", "z")
SIZES = {"xh": 2, "y": 4, "c": 2, "xl": 2, "z": 4}
bf16 = jnp.bfloat16
f32 = jnp.float32

VM = pl.BlockSpec(memory_space=pltpu.VMEM)
SM = pl.BlockSpec(memory_space=pltpu.SMEM)
ANY = pl.BlockSpec(memory_space=pl.ANY)


def moved(x, axes, to):
    sizes = [SIZES[a] for a in axes]
    pairs = []
    for here in itertools.product(*[range(s) for s in sizes]):
        there = to(*here)
        a = b = 0
        for s, i, j in zip(sizes, here, there):
            a, b = a * s + i, b * s + j % s
        pairs.append((a, b))
    return lax.ppermute(x, axes, pairs)


def ring(x, axis, sign):
    if axis == "y":
        return moved(x, ("y", "c"), lambda y, c: (y + sign * (1 - 2 * c), c))
    return moved(x, ("c", "z"), lambda c, z: (c, z + sign * (1 - 2 * c)))


def cross(x, axis):
    return moved(x, (axis,), lambda i: (1 - i,))


def spread(x, pair, axis):
    across = cross(x, pair)
    a = ring(x, axis, 1)
    b = ring(x, axis, -1)
    xa = ring(across, axis, 1)
    xb = ring(across, axis, -1)
    a2 = ring(a, axis, 1)
    xa2 = ring(xa, axis, 1)
    return [x, a, b, a2, across, xa, xb, xa2]


def owners(pair, ring_at, core):
    way = 1 - 2 * core
    return [p * 4 + (ring_at + s * way) % 4 for p in (pair, 1 - pair) for s in (0, -1, 1, -2)]


def places():
    table = []
    for xh, y, c, xl, z in itertools.product(*[range(s) for s in SIZES.values()]):
        mine = [2 * o + c for o in owners(xh, y, c)]
        other = [2 * o + 1 - c for o in owners(xh, y, 1 - c)]
        table.append([*owners(xl, z, c), *mine, *other, (xh * 4 + y) * 2 + c, xl * 4 + z, *[0] * 6])
    return np.array(table, np.int32)


def plus(*terms):
    total = terms[0].astype(f32)
    for t in terms[1:]:
        total = total + t.astype(f32)
    return total.astype(bf16)


def plus_after(a, b, after):
    def kernel(a, b, out):
        out[...] = (a[...].astype(f32) + b[...].astype(f32)).astype(bf16)

    return call(kernel, "plus_after", [], [a, b], [struct(a.shape, bf16)], us=1, after=[after])[0]


def collect(own, a, b, a2, pair, axis, after=None):
    from_b = ring(b, axis, 1)
    arrived = ring(a2, axis, -1)
    step = plus(a, arrived) if after is None else plus_after(a, arrived, after)
    from_a = ring(step, axis, -1)
    return [own, from_b, from_a, cross(plus(own[1], from_b[1], from_a[1]), pair)], step


def collect_fast(near, far, pair, axis):
    r2 = ring(far[3], axis, -1)
    rb = ring(far[2], axis, 1)
    s2 = ring(near[3], axis, -1)
    sb = ring(near[2], axis, 1)
    ra = ring(plus(far[1], r2), axis, -1)
    sa = ring(plus(near[1], s2), axis, -1)
    return [near[0], sb, sa, cross(plus(far[0], rb, ra), pair)]


def nn(a, b):
    return jnp.dot(a, b, preferred_element_type=f32)


def nt(a, b):
    return lax.dot_general(a, b, (((1,), (1,)), ((), ())), preferred_element_type=f32)


def tn(a, b):
    return lax.dot_general(a, b, (((0,), (0,)), ((), ())), preferred_element_type=f32)


def lanes(shape):
    return lax.broadcasted_iota(jnp.int32, shape, len(shape) - 1)


def rows(shape):
    return lax.broadcasted_iota(jnp.int32, shape, 0)


def call(
    kernel, name, scalars, arrays, outs, scratch=(), us=3, vmem=56, far=0, far_outs=0, after=()
):
    given = len(scalars) + len(arrays)

    def run(*refs):
        kernel(*refs[:given], *refs[given + len(after) :])

    return pl.pallas_call(
        run,
        name=name,
        out_shape=outs,
        in_specs=[SM] * len(scalars) + [VM] * (len(arrays) - far) + [ANY] * (far + len(after)),
        out_specs=[ANY] * far_outs + [VM] * (len(outs) - far_outs),
        scratch_shapes=list(scratch),
        compiler_params=pltpu.CompilerParams(vmem_limit_bytes=vmem << 20),
        cost_estimate=pl.CostEstimate(
            flops=0, bytes_accessed=us * 3690000, transcendentals=0
        ),
    )(*scalars, *arrays, *after)


def struct(shape, dtype):
    return jax.ShapeDtypeStruct(shape, dtype)


def rope_tables():
    half = HD // 2
    frequency = np.power(10000.0, np.arange(half) * (-2.0 / HD))
    angles = np.arange(LEN)[:, None] * frequency[None, :]
    cosine, sine = np.cos(angles), np.sin(angles)
    return (
        np.concatenate([cosine] * 4, axis=1).astype(np.float32),
        np.concatenate([-sine, sine, -sine, sine], axis=1).astype(np.float32),
    )


def halves_swapped(x):
    first = lanes(x.shape) % HD < HD // 2
    return jnp.where(first, pltpu.roll(x, 96, 1), pltpu.roll(x, 32, 1))


def block_column(marks, j):
    return jnp.transpose(jnp.broadcast_to(marks[j : j + 1, :], (TOK, TOK)))[:, 0:1]


QB = 256


def visible_of(marks, i):
    reach = min(LEN, QB * (i + 2))
    row = jnp.concatenate([marks[j : j + 1, :] for j in range(reach // TOK)], axis=1)
    col = jnp.concatenate(
        [block_column(marks, j) for j in range(QB // TOK * i, QB // TOK * (i + 1))], axis=0
    )
    return reach, row <= col


def prepare(where, x, marks, wq, wkv, router, gain_a, gain_m, payload, small):
    payload[0:TOK, :] = x[...]
    payload[TOK : TOK + 16, :] = jnp.zeros((16, D), bf16)
    ids = jnp.where(rows((16, TOK)) == 0, marks[...].astype(f32), 0.0)
    payload[TOK : TOK + 16, 0:TOK] = ids.astype(bf16)
    rep = where[25]
    mine = pl.ds(pl.multiple_of(rep * 128, 128), 128)
    pair = lax.div(rep, 2)
    odd = jnp.full((64, 128), lax.rem(rep, 2)) == 1
    key = wkv[:, pl.ds(pl.multiple_of(pair * 128, 128), 128)].astype(f32)
    value = wkv[:, pl.ds(pl.multiple_of(512 + pair * 128, 128), 128)].astype(f32)
    key = jnp.where(odd, pltpu.roll(key, HD, 1), key)
    value = jnp.where(odd, value, pltpu.roll(value, HD, 1))
    kv = jnp.where(lanes((64, 128)) < HD, key, value).astype(bf16)
    diagonal = rows((64, 64)) == lanes((64, 64))
    gains = []
    for gain in (gain_a, gain_m):
        row = jnp.broadcast_to(gain[...].astype(f32), (64, 64))
        gains.append(jnp.sum(jnp.where(diagonal, row, 0.0), axis=1, keepdims=True))
    lane = lanes((64, 128))
    one = (rows((EXPERTS, 128)) == lanes((EXPERTS, 128))).astype(f32).astype(bf16)
    extra = tn(router[...], one)
    extra = jnp.where(lane == 32, gains[0], jnp.where(lane == 33, gains[1], extra)).astype(bf16)
    q = wq[:, mine]
    for n in range(16):
        small[n, :, 0:128] = q
        small[n, :, 128:256] = kv
        small[n, :, 256:384] = extra


def attend(rho, w, cos, sin, *refs):
    xs = refs[:8]
    norm, q_out, kv_out, attn_out, low_out, lse_out, gain_out, marks_out = refs[8:16]
    for j in range(8):
        part = jnp.transpose(w[TOK * j : TOK * (j + 1), 256:384].astype(f32))
        gain_out[0:8, TOK * j : TOK * (j + 1)] = part[32:40, :]
    gain = gain_out[0:1, :]
    for k in range(8):
        at = rho[k]
        marks_out[pl.ds(at, 1), :] = xs[k][TOK : TOK + 16, 0:TOK].astype(f32)[0:1]
        x = xs[k][0:TOK, :].astype(f32)
        inv = lax.rsqrt(jnp.mean(x * x, axis=-1, keepdims=True) + EPS)
        norm[pl.ds(pl.multiple_of(at * TOK, TOK), TOK), :] = (x * inv * gain).astype(bf16)
    marks = marks_out[...]
    pre = nn(norm[...], w[:, 0:256])
    c, s = cos[...], sin[...]
    q = pre[:, 0:128]
    q_out[...] = ((q * c + halves_swapped(q) * s) * (HD**-0.5)).astype(bf16)
    kv = pre[:, 128:256]
    is_key = lanes(kv.shape) < HD
    kv_out[...] = jnp.where(is_key, kv * c + halves_swapped(kv) * s, kv).astype(bf16)
    kvf = kv_out[...].astype(f32)
    turned = pltpu.roll(kvf, HD, 1)
    keys = jnp.where(is_key, kvf, turned).astype(bf16)
    values = jnp.where(is_key, turned, kvf).astype(bf16)
    for i in range(LEN // QB):
        reach, visible = visible_of(marks, i)
        at = slice(QB * i, QB * (i + 1))
        qi = q_out[at, :]
        first = lanes(qi.shape) < HD
        mixed, logs = [], []
        for h in range(2):
            qh = jnp.where(first == (h == 0), qi, jnp.zeros_like(qi))
            scores = jnp.where(visible, nt(qh, keys[:reach]), -1e30)
            top = jnp.max(scores, axis=-1, keepdims=True)
            e = jnp.exp(scores - top)
            total = jnp.sum(e, axis=-1, keepdims=True)
            mixed.append(nn(e.astype(bf16), values[:reach]) / total)
            logs.append(top + jnp.log(total))
        attn = jnp.where(first, mixed[0], mixed[1])
        attn_out[at, :] = attn
        low_out[at, :] = attn.astype(bf16)
        lse_out[at, :] = jnp.where(first, logs[0], logs[1])


def head_back(h, q, kv, attn, lse, grad, marks, dq, dk, dv):
    kvf = kv[...].astype(f32)
    is_key = lanes(kvf.shape) < HD
    turned = pltpu.roll(kvf, HD, 1)
    keys = jnp.where(is_key, kvf, turned).astype(bf16)
    values = jnp.where(is_key, turned, kvf).astype(bf16)
    for i in range(LEN // QB):
        reach, visible = visible_of(marks, i)
        at = slice(QB * i, QB * (i + 1))
        qi, gi = q[at, :], grad[at, :]
        mine = (lanes(qi.shape) < HD) == (h == 0)
        qh = jnp.where(mine, qi, jnp.zeros_like(qi))
        gh = jnp.where(mine, gi, jnp.zeros_like(gi))
        part = jnp.where(mine, gi.astype(f32) * attn[at, :], 0.0)
        delta = jnp.sum(part, axis=-1, keepdims=True)
        scores = nt(qh, keys[:reach])
        log = lse[at, HD * h : HD * h + 1]
        weights = jnp.where(visible, jnp.exp(scores - log), 0.0)
        low = (weights * (nt(gh, values[:reach]) - delta)).astype(bf16)
        dq[at, :] = jnp.where(mine, nn(low, keys[:reach]), dq[at, :])
        dk[:reach, :] += tn(low, qh)
        dv[:reach, :] += tn(weights.astype(bf16), gh)


def attend_back_0(q, kv, attn, lse, grad, marks_in, dq, dk, dv):
    dq[...] = jnp.zeros_like(dq)
    dk[...] = jnp.zeros_like(dk)
    dv[...] = jnp.zeros_like(dv)
    head_back(0, q, kv, attn, lse, grad, marks_in[...], dq, dk, dv)


def attend_back_1(where, cos, sin, q, kv, attn, lse, grad, marks_in, dq_in, dk_in, dv_in, w, norm, *refs):
    (wgrad, *pairs), (out, dq, dk, dv) = refs[:5], refs[5:]
    dq[...] = dq_in[...]
    dk[...] = dk_in[...]
    dv[...] = dv_in[...]
    head_back(1, q, kv, attn, lse, grad, marks_in[...], dq, dk, dv)
    c, s = cos[...], sin[...]
    g = dq[...] * (HD**-0.5)
    out[:, 0:128] = (g * c - halves_swapped(g) * s).astype(bf16)
    key = dk[...]
    key = key + pltpu.roll(key, HD, 1)
    val = dv[...]
    val = val + pltpu.roll(val, HD, 1)
    key = key * c - halves_swapped(key) * s
    out[:, 128:256] = jnp.where(lanes(key.shape) < HD, key, val).astype(bf16)
    wgrad[...] = tn(norm[...], out[...]).astype(bf16)
    for k in range(8):
        at = pl.multiple_of(where[k] * TOK, TOK)
        pairs[k % 4][k // 4] = nt(out[pl.ds(at, TOK), :], w[:, 0:256]).astype(bf16)


def to_experts(
    x, attn, routes, priority, gain, w, early, wo, low, hidden, payload, gates_out, sems
):
    copies = []
    for s in range(16):
        to = wo.at[64 * s : 64 * (s + 1), :]
        copies.append(pltpu.make_async_copy(early.at[s, 0:64, :], to, sems.at[s]))
        copies[-1].start()
    for r in range(8):
        low[:, TOK * r : TOK * (r + 1)] = attn[r]
    for copy in copies:
        copy.wait()
    h = x[...].astype(f32) + nn(low[...], wo[...])
    hidden[...] = h
    inv = lax.rsqrt(jnp.mean(h * h, axis=-1, keepdims=True) + EPS)
    normed = (h * inv * gain[1:2, :]).astype(bf16)
    payload[:, 0:D] = normed
    logits = nn(normed, w[:, 256:384])
    lane = lanes((TOK, TOK))
    member = lane == routes[:, 0:1]
    for k in range(1, TOPK):
        member = member | (lane == routes[:, k : k + 1])
    order = jnp.broadcast_to(priority[...], (TOK, TOK)).astype(f32)
    earlier = (order < jnp.transpose(order)).astype(f32).astype(bf16)
    before = nn(earlier, member.astype(f32).astype(bf16))
    kept = member & (before < CAP)
    top = jnp.max(jnp.where(member, logits, -1e30), axis=-1, keepdims=True)
    e = jnp.where(member, jnp.exp(jnp.where(member, logits - top, 0.0)), 0.0)
    gates = e / jnp.sum(e, axis=-1, keepdims=True)
    gates_out[...] = gates
    high = gates.astype(bf16).astype(f32)
    rank = jnp.where(kept, before, -1.0)
    meta = jnp.where(
        lane < 32,
        rank,
        jnp.where(lane < 64, pltpu.roll(high, 32, 1), pltpu.roll(gates - high, 64, 1)),
    )
    payload[:, D : D + TOK] = jnp.transpose(meta).astype(bf16)


SLOTS = 16 * CAP


def assignment(pair, xb, meta, first, gate_col, at):
    two = 2 * CAP
    side = rows((two, 256)) >= CAP
    place = (rows((two, 256)) - jnp.where(side, CAP, 0)).astype(f32)
    here = side == (lanes((two, 256)) >= TOK)
    chosen = []
    for n, k in enumerate(pair):
        meta[TOK * n : TOK * (n + 1), :] = xb[k, :, D : D + TOK].astype(f32)
    for e in range(2):
        def line(offset):
            return jnp.concatenate(
                [meta[pl.ds(TOK * n + offset + first + e, 1), :] for n in range(2)], axis=1
            )

        pick = jnp.where((line(0) == place) & here, 1.0, 0.0)
        gate_col[e, at, :] = jnp.sum(pick * (line(32) + line(64)), axis=-1, keepdims=True)
        chosen.append(pick.astype(bf16))
    return jnp.concatenate(chosen, axis=0)


def fetches(who, xs, xb, x_sem, early, cb, c_sem):
    x_in = [pltpu.make_async_copy(xs[k], xb.at[k], x_sem.at[k]) for k in range(16)]
    c_in = []
    for k in range(16):
        source = early.at[who[8 + k], 64:192, :]
        c_in.append(pltpu.make_async_copy(source, cb.at[k], c_sem.at[k]))
    return x_in, c_in


def experts(who, *refs):
    xs, (w_in_far, w_out_far, cot_far) = refs[:16], refs[16:19]
    sums_far, (parts, own_r, other_r), sums = refs[19:23], refs[23:26], refs[26:30]
    act_o, pre_g, outs, picks, disp, out_g = refs[30:36]
    w_in, w_out, xb, cb, meta, cot_rows, gate_col, back, gg = refs[36:45]
    x_sem, c_sem, w_sem, o_sem, r_sem, g_sem = refs[45:]
    first = who[24] * 2
    two = 2 * CAP
    x_in, c_in = fetches(who, xs, xb, x_sem, cot_far, cb, c_sem)
    w_copies = []
    for e in range(2):
        w_copies.append(pltpu.make_async_copy(w_in_far.at[e], w_in.at[e], w_sem.at[2 * e]))
        w_copies.append(pltpu.make_async_copy(w_out_far.at[e], w_out.at[e], w_sem.at[2 * e + 1]))
    for p in range(8):
        x_in[p].start()
        x_in[p + 8].start()
    w_copies[0].start()
    w_copies[1].start()
    for p in range(8):
        c_in[p].start()
        c_in[p + 8].start()
    w_copies[2].start()
    w_copies[3].start()
    leaving = []

    def leave(source, to, sem):
        leaving.append(pltpu.make_async_copy(source, to, sem))
        leaving[-1].start()

    for p in range(8):
        at = slice(two * p, two * (p + 1))
        pair = (p, p + 8)
        for k in pair:
            x_in[k].wait()
        pick = assignment(pair, xb, meta, first, gate_col, at)
        picks[p] = pick
        found = nn(pick, jnp.concatenate([xb[k, :, 0:D] for k in pair], axis=0)).astype(bf16)
        for e in range(2):
            disp[e, at, :] = found[two * e : two * (e + 1)]
    for e in range(2):
        w_copies[2 * e].wait()
        pre = nn(disp[e], w_in[e])
        gate, up = pre[:, 0:F], pre[:, F : 2 * F]
        sig = 1.0 / (1.0 + jnp.exp(-gate))
        silu = gate * sig
        act = (silu * up).astype(bf16)
        act_o[e] = act
        w_copies[2 * e + 1].wait()
        out = nn(act, w_out[e])
        if e == 0:
            for p in range(8):
                at = slice(two * p, two * (p + 1))
                c_in[p].wait()
                c_in[p + 8].wait()
                cot = nn(picks[p], jnp.concatenate([cb[p], cb[p + 8]], axis=0))
                for n in range(2):
                    part = cot[two * n : two * (n + 1)]
                    cot_rows[n, at, :] = part.astype(bf16)
                    out_g[n, at, :] = (gate_col[n, at, :] * part).astype(bf16)
        g = jnp.sum(out * cot_rows[e].astype(f32), axis=-1, keepdims=True)
        high = g.astype(bf16).astype(f32)
        lane = lanes((SLOTS, TOK))
        gg[e] = jnp.where(
            lane == first + e, high, jnp.where(lane == first + e + 32, g - high, 0.0)
        ).astype(bf16)
        outs[e] = (gate_col[e] * out).astype(bf16)
        act_grad = nt(out_g[e], w_out[e])
        d_up = act_grad * silu
        d_gate = act_grad * up * (sig * (1.0 + gate * (1.0 - sig)))
        pre_g[e, :, 0:F] = d_gate.astype(bf16)
        pre_g[e, :, F : 2 * F] = d_up.astype(bf16)
        back[e] = nt(pre_g[e], w_in[e]).astype(bf16)
    for half in (1, 0):
        for p in range(4 * half, 4 * half + 4):
            at = slice(two * p, two * (p + 1))
            slot = jnp.concatenate([back[0, at, :], back[1, at, :]], axis=0)
            grads = jnp.concatenate([gg[0, at, :], gg[1, at, :]], axis=0)
            for n in range(2):
                whole = sums[2 * half + n].at[p % 4]
                pick = picks[p, :, TOK * n : TOK * (n + 1)]
                whole[:, 0:D] = tn(pick, slot).astype(bf16)
                whole[:, D : D + TOK] = tn(pick, grads).astype(bf16)
        for n in (2 * half + 1, 2 * half):
            leave(sums[n], sums_far[n], o_sem.at[n])
    for p in range(8):
        at = slice(two * p, two * (p + 1))
        value = jnp.concatenate([outs[0, at, :], outs[1, at, :]], axis=0)
        for n, to in enumerate((own_r, other_r)):
            k = p + 8 * n
            cb[k] = tn(picks[p, :, TOK * n : TOK * (n + 1)], value).astype(bf16)
            leave(cb.at[k], to.at[p % 4, p // 4], r_sem.at[k])

    far = who[25] // 4

    def send(grad, e, count, row):
        for k in range(8):
            to = parts.at[2 * (k % 4) + lax.bitwise_xor(k // 4, far), row : row + count, :]
            sem = g_sem.at[e, k + 8 * (count == 64)]
            leave(grad.at[e, count * k : count * (k + 1), :], to, sem)

    for e in range(2):
        w_in[e] = tn(disp[e], pre_g[e]).astype(bf16)
        send(w_in, e, TOK, TOK * e)
        w_out[e] = tn(act_o[e], out_g[e]).astype(bf16)
        send(w_out, e, 64, 256 + 64 * e)
    for copy in leaving:
        copy.wait()


def second_half(whole, after):
    def kernel(a, _, out):
        out[...] = a[...]

    return pl.pallas_call(
        kernel,
        name="second_half",
        out_shape=struct((384, D), bf16),
        grid=(1,),
        in_specs=[pl.BlockSpec((384, D), lambda i: (1, 0)), ANY],
        out_specs=pl.BlockSpec((384, D), lambda i: (0, 0)),
    )(whole, after)


def expert_grads(a, b, grad_in, grad_out):
    for e in range(2):
        at = slice(TOK * e, TOK * (e + 1))
        grad_in[e] = a[at, :].astype(f32) + b[at, :].astype(f32)
        at = slice(256 + 64 * e, 320 + 64 * e)
        grad_out[e] = a[at, :].astype(f32) + b[at, :].astype(f32)


def added(a, b, name, us=2):
    count = a.shape[0]

    def kernel(a_ref, b_ref, *outs):
        for n, out in enumerate(outs):

            @pl.when(pl.program_id(0) == n)
            def _(out=out):
                out[...] = (a_ref[0].astype(f32) + b_ref[0].astype(f32)).astype(bf16)

    zeros = (0,) * (a.ndim - 1)
    block = pl.BlockSpec((1, *a.shape[1:]), lambda i: (i, *zeros))
    return pl.pallas_call(
        kernel,
        name=name,
        out_shape=[struct(a.shape[1:], bf16)] * count,
        grid=(count,),
        in_specs=[block, block],
        out_specs=[pl.BlockSpec(a.shape[1:], lambda i: zeros)] * count,
        compiler_params=pltpu.CompilerParams(vmem_limit_bytes=32 << 20),
        cost_estimate=pl.CostEstimate(
            flops=0, bytes_accessed=us * 3690000, transcendentals=0
        ),
    )(a, b)


def layer_result(hidden, t0, t1, t2, t3, result):
    total = t0[0].astype(f32) + t1[0].astype(f32) + t2[0].astype(f32) + t3[...].astype(f32)
    result[...] = (hidden[...] + total).astype(bf16)


def last_terms(wgrad, t0, t1, t2, t3, last):
    total = t0[0].astype(f32) + t1[0].astype(f32) + t2[0].astype(f32) + t3[...].astype(f32)
    last[:, 0 : D + TOK] = total.astype(bf16)
    last[:, D + TOK :] = sum(wgrad[n].astype(f32) for n in range(16)).astype(bf16)


def from_experts(where, t0, t1, t2, t3, gates, hidden, cot, gain, w, wo, attn_low, payload, *refs):
    attn_grad, hidden_grad, own, other, whole = refs
    total = t0[...].astype(f32) + t1[...].astype(f32) + t2[...].astype(f32) + t3[...].astype(f32)
    lane = lanes((TOK, TOK))
    g = total[:, D : D + TOK]
    g = jnp.where(lane < 32, g + pltpu.roll(g, 96, 1), 0.0)
    gate = gates[...]
    picked = gate * (g - jnp.sum(gate * g, axis=-1, keepdims=True))
    low = picked.astype(bf16)
    grad = total[:, 0:D] + nt(low, w[:, 256:384])
    h = hidden[...]
    r = lax.rsqrt(jnp.mean(h * h, axis=-1, keepdims=True) + EPS)
    gain_row = jnp.sum(grad * h * r, axis=0, keepdims=True)
    scaled = grad * gain[1:2, :]
    dot = jnp.mean(h * scaled, axis=-1, keepdims=True)
    out = cot[...].astype(f32) + r * scaled - h * (r * r * r * dot)
    hidden_grad[...] = out
    b = out.astype(bf16)
    ag = nt(b, wo[...]).astype(bf16)
    for j in range(8):
        attn_grad[j] = ag[:, TOK * j : TOK * (j + 1)]
    whole[:, 0:D] = tn(attn_low[...], b).astype(bf16)
    router = tn(payload[:, 0:D], low)
    for j in range(8):
        at = slice(TOK * j, TOK * (j + 1))
        col = jnp.transpose(jnp.broadcast_to(gain_row[:, at], (TOK, TOK)))
        whole[at, D : D + TOK] = jnp.where(lane == 32, col, router[at, :]).astype(bf16)
    for k in range(8):
        for n, to in enumerate((own, other)):
            at = pl.multiple_of(where[8 + k + 8 * n] * 64, 64)
            to[k % 4, k // 4] = whole[pl.ds(at, 64), :]


def to_input(x, gain, hidden_grad, t0, t1, t2, t3, out):
    grad = t0[0].astype(f32) + t1[0].astype(f32) + t2[0].astype(f32) + t3[...].astype(f32)
    h = x[...].astype(f32)
    r = lax.rsqrt(jnp.mean(h * h, axis=-1, keepdims=True) + EPS)
    scaled = grad * gain[0:1, :]
    dot = jnp.mean(h * scaled, axis=-1, keepdims=True)
    out[...] = hidden_grad[...] + r * scaled - h * (r * r * r * dot)


def column_as_row(column):
    return jnp.transpose(jnp.broadcast_to(column, (64, TOK)))[0:1, :]


def finished(rho, wq, wkv, gain, *refs):
    parts = refs[:8]
    out_q, out_kv, out_o, out_router, out_moe, out_gain, pairs = refs[8:]
    total = jnp.zeros((64, D + TOK), f32)
    for k in range(8):
        total = total + parts[k][:, 0 : D + TOK].astype(f32)
        at = rho[k]
        out_q[:, pl.ds(pl.multiple_of(at * TOK, TOK), TOK)] = parts[k][
            :, D + TOK : D + 2 * TOK
        ].astype(f32)
        pairs[at] = parts[k][:, D + 2 * TOK : D + 3 * TOK].astype(f32)
    out_o[...] = total[:, 0:D]
    out_router[...] = jnp.transpose(total[:, D : D + TOK])[0:EXPERTS, :]
    out_moe[...] = column_as_row(total[:, D + EXPERTS : D + EXPERTS + 1])
    first = lanes((64, TOK)) < HD
    for j in range(4):
        a, b = pairs[2 * j], pairs[2 * j + 1]
        out_kv[:, TOK * j : TOK * (j + 1)] = jnp.where(first, a, pltpu.roll(b, HD, 1))
        out_kv[:, 512 + TOK * j : 512 + TOK * (j + 1)] = jnp.where(first, pltpu.roll(a, HD, 1), b)
    both = out_q[...] * wq[...].astype(f32) + out_kv[...] * wkv[...].astype(f32)
    out_gain[...] = column_as_row(jnp.sum(both, axis=-1, keepdims=True)) / gain[...].astype(f32)


def body(
    layer_input,
    cotangent,
    gain_attn,
    w_query,
    w_keyval,
    w_output,
    gain_moe,
    w_router,
    w_in,
    w_out,
    routes,
    priority,
    block_ids,
):
    x = layer_input.reshape(TOK, D)
    cot = cotangent.reshape(TOK, D)
    route_rows = routes.reshape(TOK, TOPK)
    order_row = priority.reshape(1, TOK)
    marks = block_ids.reshape(1, TOK)
    where = lax.dynamic_index_in_dim(
        jnp.asarray(places()), lax.axis_index(tuple(SIZES)), keepdims=False
    )

    payload, small = call(
        prepare,
        "prepare",
        [where],
        [
            x,
            block_ids.reshape(1, TOK),
            w_query,
            w_keyval,
            w_router.T,
            gain_attn.reshape(1, 64),
            gain_moe.reshape(1, 64),
        ],
        [struct((TOK + 16, D), bf16), struct((16, 64, 384), bf16)],
        us=2,
    )
    xs = spread(payload, "xl", "z")
    small = lax.all_to_all(small, SHARD, 0, 0, tiled=True).reshape(D, 384)
    early = lax.all_gather(jnp.concatenate([w_output, cot], axis=0), SHARD, axis=0)
    cos, sin = (jnp.asarray(t) for t in rope_tables())
    norm, q, kv, attn, low_cols, lse, gain, seq_marks = call(
        attend,
        "attend",
        [where],
        [small, cos, sin, *xs],
        [
            struct((LEN, D), bf16),
            struct((LEN, 128), bf16),
            struct((LEN, 128), bf16),
            struct((LEN, 128), f32),
            struct((LEN, 128), bf16),
            struct((LEN, 128), f32),
            struct((8, D), f32),
            struct((8, TOK), f32),
        ],
        us=10,
    )
    attn_in = lax.all_to_all(low_cols.reshape(8, TOK, 128), REP, 0, 0, tiled=True)
    wo, low, hidden, payload, gates = call(
        to_experts,
        "to_experts",
        [],
        [x, attn_in, route_rows, order_row, gain, small, early],
        [
            struct((D, D), bf16),
            struct((TOK, D), bf16),
            struct((TOK, D), f32),
            struct((TOK, D + TOK), bf16),
            struct((TOK, TOK), f32),
        ],
        [pltpu.SemaphoreType.DMA((16,))],
        far=1,
        us=5,
    )
    tokens = spread(payload, "xh", "y")
    tokens = tokens + [cross(t, "c") for t in tokens]
    sums = [struct((4, TOK, D + TOK), bf16)] * 4
    own_0, other_0, own_1, other_1, parts, own_r, other_r = call(
        experts,
        "experts",
        [where],
        [*tokens, w_in, w_out, early],
        [*sums, struct((8, 384, D), bf16), *[struct((4, 2, TOK, D), bf16)] * 2],
        [
            *[pltpu.VMEM(k.shape, k.dtype) for k in sums],
            pltpu.VMEM((2, SLOTS, F), bf16),
            pltpu.VMEM((2, SLOTS, 2 * F), bf16),
            pltpu.VMEM((2, SLOTS, D), bf16),
            pltpu.VMEM((8, 4 * CAP, 256), bf16),
            pltpu.VMEM((2, SLOTS, D), bf16),
            pltpu.VMEM((2, SLOTS, D), bf16),
            pltpu.VMEM((2, D, 2 * F), bf16),
            pltpu.VMEM((2, F, D), bf16),
            pltpu.VMEM((16, TOK, D + TOK), bf16),
            pltpu.VMEM((16, TOK, D), bf16),
            pltpu.VMEM((256, TOK), f32),
            pltpu.VMEM((2, SLOTS, D), bf16),
            pltpu.VMEM((2, SLOTS, 1), f32),
            pltpu.VMEM((2, SLOTS, D), bf16),
            pltpu.VMEM((2, SLOTS, TOK), bf16),
            pltpu.SemaphoreType.DMA((16,)),
            pltpu.SemaphoreType.DMA((16,)),
            pltpu.SemaphoreType.DMA((4,)),
            pltpu.SemaphoreType.DMA((4,)),
            pltpu.SemaphoreType.DMA((16,)),
            pltpu.SemaphoreType.DMA((2, 16)),
        ],
        us=27,
        vmem=60,
        far=19,
        far_outs=7,
    )
    far = added(own_1, cross(other_1, "c"), "far_sums")
    near = added(own_0, cross(other_0, "c"), "near_sums")
    slot_terms = collect_fast(near, far, "xh", "y")
    r_pairs = added(own_r, cross(other_r, "c"), "result_sums", us=4)
    r_terms, r_step = collect(*r_pairs, "xh", "y")
    expert_sum = lax.psum_scatter(parts.reshape(-1, D), "z", scatter_dimension=0, tiled=True)
    attn_grad, hidden_grad, dense_own, dense_other = call(
        from_experts,
        "from_experts",
        [where],
        [*slot_terms, gates, hidden, cot, gain, small, wo, low, payload],
        [
            struct((8, TOK, 128), bf16),
            struct((TOK, D), f32),
            *[struct((4, 2, 64, D + TOK), bf16)] * 2,
        ],
        [pltpu.VMEM((D, D + TOK), bf16)],
        us=6,
        after=[r_pairs[0]],
    )
    attn_grad = lax.all_to_all(attn_grad, REP, 0, 0, tiled=True).reshape(LEN, 128)
    dense = added(dense_own, cross(dense_other, "c"), "dense_sums", us=3)
    dense_terms, dense_step = collect(*dense, "xh", "y")
    first = call(
        attend_back_0,
        "attend_back_0",
        [],
        [q, kv, attn, lse, attn_grad, seq_marks],
        [struct((LEN, 128), f32)] * 3,
        us=60,
    )
    expert_in = cross(second_half(expert_sum, first[0]), "xl")
    wgrad, *norm_terms = call(
        attend_back_1,
        "attend_back_1",
        [where],
        [cos, sin, q, kv, attn, lse, attn_grad, seq_marks, *first, small, norm],
        [struct((D, 256), bf16), *[struct((2, TOK, D), bf16)] * 4],
        [pltpu.VMEM((LEN, 256), bf16), *[pltpu.VMEM((LEN, 128), f32)] * 3],
        us=10,
        after=[dense_step],
    )
    wgrad = lax.all_to_all(wgrad.reshape(16, 64, 256), SHARD, 0, 0, tiled=True)
    norm_terms, norm_step = collect(*norm_terms, "xl", "z", expert_in)
    result = call(
        layer_result, "layer_result", [], [hidden, *r_terms], [struct((TOK, D), bf16)]
    )[0]
    grad_in, grad_out = call(
        expert_grads,
        "expert_grads",
        [],
        [expert_in, expert_sum],
        [struct((2, TOK, D), f32), struct((2, 64, D), f32)],
    )
    last = call(
        last_terms,
        "last_terms",
        [],
        [wgrad, *dense_terms],
        [struct((64, D + 3 * TOK), bf16)],
        after=[norm_step, result, expert_in],
        us=2,
    )[0]
    last = spread(last, "xl", "z")
    grad_input = call(
        to_input,
        "to_input",
        [],
        [x, gain, hidden_grad, *norm_terms],
        [struct((TOK, D), f32)],
    )[0]
    grad_q, grad_kv, grad_o, grad_router, grad_moe, grad_gain = call(
        finished,
        "finished",
        [where],
        [w_query, w_keyval, gain_attn.reshape(1, 64), *last],
        [
            struct((64, D), f32),
            struct((64, D), f32),
            struct((64, D), f32),
            struct((EXPERTS, 64), f32),
            struct((1, 64), f32),
            struct((1, 64), f32),
        ],
        [pltpu.VMEM((8, 64, TOK), f32)],
        after=[grad_input, grad_in],
    )
    return (
        result.reshape(layer_input.shape),
        grad_input.reshape(layer_input.shape),
        grad_gain.reshape(64),
        grad_q,
        grad_kv,
        grad_o,
        grad_moe.reshape(64),
        grad_router.T,
        grad_in,
        grad_out,
    )


def solution(mesh):
    split = Mesh(mesh.devices.reshape(tuple(SIZES.values())), tuple(SIZES))
    tokens = P(SHARD, REP, None)
    weight = P(SHARD, None)
    return jax.shard_map(
        body,
        mesh=split,
        in_specs=(
            tokens,
            tokens,
            P(SHARD),
            weight,
            weight,
            weight,
            P(SHARD),
            weight,
            P(SHARD, None, None),
            P(SHARD, None, None),
            tokens,
            tokens,
            P(SHARD, REP),
        ),
        out_specs=(
            tokens,
            tokens,
            P(SHARD),
            weight,
            weight,
            weight,
            P(SHARD),
            weight,
            tokens,
            tokens,
        ),
        check_vma=False,
    )
```
